256 devices in a mesh: gx: 16 (over x, z_hi), gy: 16 (over z_lo, y, core).
Axes of the slice: x: 4, y: 4, z: 8 (z_hi: 4, z_lo: 2; z = z_hi * 2 + z_lo), core: 2. Of those that a mesh axis runs over, the one named last changes fastest.
Arguments:
- phase_start: float32 [384, 256, 256], P('gx', 'gy'), may hold values from 0 to 1
- potential_start: float32 [384, 256, 256], P('gx', 'gy'), may hold values from -6 to 6
- phase_cotangent: float32 [384, 256, 256], P('gx', 'gy'), may hold values from -6 to 6
- potential_cotangent: float32 [384, 256, 256], P('gx', 'gy'), may hold values from -6 to 6
- orientation: int32 [384, 256, 256], P('gx', 'gy'), may hold values from 0 to 7
- anisotropy_index: int32 [384, 256, 256], P('gx', 'gy'), may hold values from 0 to 15
- boundary_mask: int32 [384, 256, 256], P('gx', 'gy'), may hold values 0 or 1
- stiffness_table: float32 [16], replicated, may hold values from 0.2 to 1.2
- partition_table: float32 [8], replicated, may hold values from 0.1 to 0.9
Outputs:
- phase_gradient: float32 [384, 256, 256], P('gx', 'gy')
- potential_gradient: float32 [384, 256, 256], P('gx', 'gy')
The draws below stay inside these ranges and needn't reach their ends.
All inputs are finite; a program needn't handle non-finite values. No bound on the sum of `boundary_mask` on one device may be relied on, other than what follows from the above.
Results may differ from the reference program's by a relative error of at most 0.000062.
Values sent between devices are 32-bit elements; how exact they have to be, the bound alone decides.
A program may use at most 64 MiB of HBM per device.

```python
import math
import jax
import jax.numpy as jnp

CZ = 256
NCLASS = 8
NANISO = 16
NX = 384
NY = 256


def place_ends(result, stream_key, smallest, largest):
    place = [jax.random.randint(jax.random.fold_in(stream_key, axis), (), 0, length) for axis, length in enumerate(result.shape)]
    widest = result.shape.index(max(result.shape))
    beside = place[:widest] + [(place[widest] + 1) % result.shape[widest]] + place[widest + 1:]
    return result.at[tuple(place)].set(smallest).at[tuple(beside)].set(largest)


def levels(rng, dims, split, smallest, largest):
    gain = 1.0
    for position, parts in split:
        steps = jax.random.uniform(jax.random.fold_in(jax.random.fold_in(rng, 6), position), (parts,), jnp.float32, smallest / len(split), largest / len(split))
        gain = gain * jnp.repeat(jnp.exp(steps), dims[position] // parts).reshape((-1,) + (1,) * (len(dims) - 1 - position))
    return gain


def noise(rng, extent, scale, reach, cuts=(), held_as=jnp.bfloat16):
    drawn = scale * jax.random.normal(rng, extent, jnp.float32)
    if cuts:
        drawn = drawn * levels(rng, extent, cuts, -0.22, 0.18)
    return jnp.clip(drawn, -reach, reach).astype(held_as)


def setup_inputs(seed: int = 0) -> dict:
    splits = jax.random.split(jax.random.key(seed), 10)
    return {
        "phase_start": jnp.clip(1.0 * jax.random.uniform(splits[0], (NX, NY, CZ), jnp.float32) ** levels(splits[0], (NX, NY, CZ), ((0, 16), (1, 16)), -0.2, 0.2), 0.0, 1.0),
        "potential_start": noise(splits[1], (NX, NY, CZ), 1.0, 6.0, ((0, 16), (1, 16)), jnp.float32),
        "phase_cotangent": noise(splits[2], (NX, NY, CZ), 1.0, 6.0, ((0, 16), (1, 16)), jnp.float32),
        "potential_cotangent": noise(splits[3], (NX, NY, CZ), 1.0, 6.0, ((0, 16), (1, 16)), jnp.float32),
        "orientation": place_ends(jax.random.randint(splits[4], (NX, NY, CZ), 0, NCLASS), jax.random.fold_in(splits[4], 1), 0, NCLASS - 1).astype(jnp.int32),
        "anisotropy_index": place_ends(jax.random.randint(splits[5], (NX, NY, CZ), 0, NANISO), jax.random.fold_in(splits[5], 1), 0, NANISO - 1).astype(jnp.int32),
        "boundary_mask": place_ends((jax.random.randint(splits[6], (NX, NY, CZ), 0, 8) < 1).astype(jnp.int32), jax.random.fold_in(splits[6], 1), 0, 1),
        "stiffness_table": jnp.clip(jnp.exp(jax.random.uniform(splits[7], (NANISO,), jnp.float32, math.log(0.2), math.log(1.2))), 0.2, 1.2),
        "partition_table": jnp.clip(jax.random.uniform(splits[8], (NCLASS,), jnp.float32, 0.1, 0.9), 0.1, 0.9),
    }


mobility_step = 0.1
well_height = 1.0
coupling = 1.0
diffusion_step = 0.03

def laplacian(field):
    padded = jnp.pad(field, 1)
    beside = padded[2:, 1:-1, 1:-1] + padded[:-2, 1:-1, 1:-1]
    beside = beside + padded[1:-1, 2:, 1:-1] + padded[1:-1, :-2, 1:-1]
    beside = beside + padded[1:-1, 1:-1, 2:] + padded[1:-1, 1:-1, :-2]
    return beside - 6.0 * field

def reaction(phase, potential, lap_phase, lap_potential, stiffness, jump, movable):
    denominator = phase * phase + (1.0 - phase) * (1.0 - phase)
    interp = phase * phase / denominator
    slope = 2.0 * phase * (1.0 - phase) / (denominator * denominator)
    drive = stiffness * lap_phase - 2.0 * well_height * phase * (1.0 - phase) * (1.0 - 2.0 * phase) + coupling * jump * slope * potential
    phase_next = phase + movable * mobility_step * drive
    potential_next = potential + movable * (diffusion_step * lap_potential - jump * slope * (phase_next - phase)) / (1.0 - jump * interp)
    return (phase_next, potential_next)

def reference(phase_start, potential_start, phase_cotangent, potential_cotangent, orientation, anisotropy_index, boundary_mask, stiffness_table, partition_table):
    stiffness = stiffness_table[anisotropy_index]
    jump = 1.0 - partition_table[orientation]
    movable = 1.0 - boundary_mask.astype(jnp.float32)

    def forward(phase, potential):
        for step in range(2):
            phase, potential = reaction(phase, potential, laplacian(phase), laplacian(potential), stiffness, jump, movable)
        return (phase, potential)
    outputs, pullback = jax.vjp(forward, phase_start, potential_start)
    phase_gradient, potential_gradient = pullback((phase_cotangent, potential_cotangent))
    return (phase_gradient, potential_gradient)
```

```python
import functools

import jax
import jax.numpy as jnp
from jax import lax
from jax.experimental import pallas as pl
from jax.experimental.pallas import tpu as pltpu
from jax.sharding import PartitionSpec as P

mobility_step = 0.1
well_height = 1.0
coupling = 1.0
diffusion_step = 0.03

MESH = pl.DeviceIdType.MESH


def pick(index, table, count):
    values = [table[k] for k in range(count)]
    bit = 1
    while len(values) > 1:
        odd = (index & bit) != 0
        values = [jnp.where(odd, values[k + 1], values[k]) for k in range(0, len(values), 2)]
        bit *= 2
    return values[0]


def local_terms(phase, jump):
    t = phase - phase * phase
    inverse = 1.0 / (1.0 - 2.0 * t)
    slope = 2.0 * t * inverse * inverse
    slope_derivative = 2.0 * (1.0 - 2.0 * phase) * (1.0 + 2.0 * t) * (inverse * inverse * inverse)
    release = 1.0 / (1.0 - jump * (phase * phase * inverse))
    return t, slope, slope_derivative, release


def kernel(
    nx_dev, ny_dev,
    p_hbm, m_hbm, a_hbm, b_hbm, or_hbm, an_hbm, bm_hbm, st, pt,
    out_p, out_m,
    P0, M0, A, B, OR, AN, BM, P1, M1, U1, V1, U0, V0,
    KAP, JMP, MOV, JS0, W0, G0, K0,
    load_sem, ss, rs,
):
    X, Y, Z = p_hbm.shape
    HI, LO = Y, Y + 7
    gx, gy = lax.axis_index("gx"), lax.axis_index("gy")
    has = {
        ("x", 0): gx > 0, ("x", 1): gx < nx_dev - 1,
        ("y", 0): gy > 0, ("y", 1): gy < ny_dev - 1,
    }
    device = {
        ("x", 0): {"gx": gx - 1}, ("x", 1): {"gx": gx + 1},
        ("y", 0): {"gy": gy - 1}, ("y", 1): {"gy": gy + 1},
    }

    loads = []
    for k, (src, dst, off) in enumerate((
        (p_hbm, P0, 2), (m_hbm, M0, 2), (or_hbm, OR, 1), (an_hbm, AN, 1),
        (bm_hbm, BM, 1), (a_hbm, A, 1), (b_hbm, B, 1),
    )):
        copy = pltpu.make_async_copy(src, dst.at[pl.ds(off, X), pl.ds(0, Y), :], load_sem.at[k])
        copy.start()
        loads.append(copy)

    barrier = pltpu.get_barrier_semaphore()
    count = jnp.int32(0)
    for key, there in has.items():
        @pl.when(there)
        def _():
            pl.semaphore_signal(barrier, inc=1, device_id=device[key], device_id_type=MESH)
        count = count + there.astype(jnp.int32)

    for side, (two, one) in enumerate(((0, 0), (X + 2, X + 1))):
        @pl.when(jnp.logical_not(has["x", side]))
        def _():
            for ref in (P0, M0):
                ref[pl.ds(two, 2)] = jnp.zeros((2,) + ref.shape[1:], ref.dtype)
            for ref in (A, B, OR, AN):
                ref[one] = jnp.zeros(ref.shape[1:], ref.dtype)
            BM[one] = jnp.ones(BM.shape[1:], BM.dtype)
            for ref in (U0, V0):
                ref[one] = jnp.zeros(ref.shape[1:], ref.dtype)
    for side, row in enumerate((LO, HI)):
        @pl.when(jnp.logical_not(has["y", side]))
        def _():
            for ref, off in ((P0, 2), (M0, 2), (P1, 1), (M1, 1), (U1, 1), (V1, 1), (U0, 1), (V0, 1)):
                ref[pl.ds(off, X), pl.ds(row, 1), :] = jnp.zeros((X, 1, Z), ref.dtype)

    sems = iter(range(ss.shape[0]))

    def exchange(axis, pieces):
        sends = {0: [], 1: []}
        arrivals = {0: [], 1: []}
        for ref, down, down_to, up, up_to in pieces:
            for side, src, dst in ((0, down, down_to), (1, up, up_to)):
                k = next(sems)
                copy = pltpu.make_async_remote_copy(
                    src_ref=ref.at[src], dst_ref=ref.at[dst], send_sem=ss.at[k], recv_sem=rs.at[k],
                    device_id=device[axis, side], device_id_type=MESH,
                )
                sends[side].append(copy)
                arrivals[1 - side].append(copy)

        def start():
            for side in (0, 1):
                @pl.when(has[axis, side])
                def _():
                    for copy in sends[side]:
                        copy.start()

        def wait_recv():
            for side in (0, 1):
                @pl.when(has[axis, side])
                def _():
                    for copy in arrivals[side]:
                        copy.wait_recv()

        def wait_send():
            for side in (0, 1):
                @pl.when(has[axis, side])
                def _():
                    for copy in sends[side]:
                        copy.wait_send()

        return start, wait_recv, wait_send

    rows = pl.ds(0, Y)

    def x_layers(ref, off, width):
        return (
            ref,
            (pl.ds(off, width), rows), (pl.ds(off + X, width), rows),
            (pl.ds(off + X - width, width), rows), (pl.ds(off - width, width), rows),
        )

    def y_rows(ref, off):
        own = pl.ds(off, X)
        return ref, (own, 0), (own, HI), (own, Y - 1), (own, LO)

    def corner(ref):
        tile = pl.ds(Y, 8)
        return ref, (2, tile), (X + 2, tile), (X + 1, tile), (1, tile)

    x_state = exchange("x", [x_layers(ref, 2, 2) for ref in (P0, M0)])
    y_state = exchange("y", [y_rows(ref, 2) for ref in (P0, M0)])
    x_rest = exchange("x", [x_layers(ref, 1, 1) for ref in (OR, AN, BM, A, B)])
    x_corner = exchange("x", [corner(ref) for ref in (P0, M0)])
    y_middle = exchange("y", [y_rows(ref, 1) for ref in (P1, M1, U1, V1)])
    x_last = exchange("x", [x_layers(ref, 1, 1) for ref in (U0, V0)])
    y_last = exchange("y", [y_rows(ref, 1) for ref in (U0, V0)])

    loads[0].wait()
    loads[1].wait()
    pl.semaphore_wait(barrier, count)
    x_state[0]()
    y_state[0]()
    for copy in loads[2:]:
        copy.wait()
    x_rest[0]()

    lane = lax.broadcasted_iota(jnp.int32, (Y, Z), 1)
    first, last = lane == 0, lane == Z - 1

    def lap(ref, i):
        wide = ref[i]
        center = wide[:Y]
        beside = ref[i - 1, :Y] + ref[i + 1, :Y]
        beside = beside + pltpu.roll(wide, Y + 7, 0)[:Y] + pltpu.roll(wide, 1, 0)[:Y]
        beside = beside + jnp.where(first, 0.0, pltpu.roll(center, 1, 1))
        beside = beside + jnp.where(last, 0.0, pltpu.roll(center, Z - 1, 1))
        return beside - 6.0 * center

    def tables(x):
        i = x + 1
        KAP[i] = pick(AN[i], st, st.shape[0])
        JMP[i] = 1.0 - pick(OR[i], pt, pt.shape[0])
        MOV[i] = 1.0 - BM[i].astype(jnp.float32)

    def forward(x, own):
        i = x + 1
        phase, potential = P0[x + 2, :Y], M0[x + 2, :Y]
        lap_phase, lap_potential = lap(P0, x + 2), lap(M0, x + 2)
        stiffness, jump, movable = KAP[i], JMP[i], MOV[i]
        t, slope, slope_derivative, release = local_terms(phase, jump)
        held_slope = jump * slope
        drive = (
            stiffness * lap_phase
            - 2.0 * well_height * t * (1.0 - 2.0 * phase)
            + coupling * held_slope * potential
        )
        step = movable * mobility_step * drive
        flux = (diffusion_step * lap_potential - held_slope * step) * release
        phase_next = phase + step
        potential_next = potential + movable * flux
        P1[i, :Y] = phase_next
        M1[i, :Y] = potential_next
        if own:
            JS0[x] = held_slope
            W0[x] = movable * release
            G0[x] = well_height * (12.0 * t - 2.0) + coupling * jump * slope_derivative * potential
            K0[x] = jump * (slope * flux - step * slope_derivative)
        _, slope, _, release = local_terms(phase_next, jump)
        spread = B[i] * (movable * release)
        pull = mobility_step * movable * (A[i] - spread * (jump * slope))
        U1[i, :Y] = stiffness * pull
        V1[i, :Y] = diffusion_step * spread

    def backward(x):
        i = x + 1
        phase, potential = P1[i, :Y], M1[i, :Y]
        stiffness, jump, movable = KAP[i], JMP[i], MOV[i]
        t, slope, slope_derivative, release = local_terms(phase, jump)
        held_slope = jump * slope
        drive = (
            stiffness * lap(P1, i)
            - 2.0 * well_height * t * (1.0 - 2.0 * phase)
            + coupling * held_slope * potential
        )
        step = movable * mobility_step * drive
        flux = (diffusion_step * lap(M1, i) - held_slope * step) * release
        gain = well_height * (12.0 * t - 2.0) + coupling * jump * slope_derivative * potential
        keep = jump * (slope * flux - step * slope_derivative)
        spread = B[i] * (movable * release)
        pull = mobility_step * movable * (A[i] - spread * held_slope)
        bar_p = A[i] + pull * gain + spread * keep + lap(U1, i)
        bar_m = B[i] + coupling * held_slope * pull + lap(V1, i)
        spread = bar_m * W0[x]
        pull = mobility_step * movable * (bar_p - spread * JS0[x])
        U0[i, :Y] = stiffness * pull
        V0[i, :Y] = diffusion_step * spread
        out_p[x] = bar_p + pull * G0[x] + spread * K0[x]
        out_m[x] = bar_m + coupling * JS0[x] * pull

    def finish(x):
        out_p[x] = out_p[x] + lap(U0, x + 1)
        out_m[x] = out_m[x] + lap(V0, x + 1)

    def over(low, high, body):
        def step(x, carry):
            body(x)
            return carry
        lax.fori_loop(low, high, step, 0)

    over(0, X, tables)
    y_state[1]()
    x_corner[0]()
    over(1, X - 1, lambda x: forward(x, True))
    x_state[1]()
    over(0, 2, lambda k: forward(k * (X - 1), True))
    y_middle[0]()
    x_rest[1]()
    x_corner[1]()
    over(0, 2, lambda k: tables(k * (X + 1) - 1))
    over(0, 2, lambda k: forward(k * (X + 1) - 1, False))
    y_middle[1]()
    over(0, 2, lambda k: backward(k * (X - 1)))
    x_last[0]()
    over(1, X - 1, backward)
    y_last[0]()
    y_last[1]()
    over(1, X - 1, finish)
    x_last[1]()
    over(0, 2, lambda k: finish(k * (X - 1)))
    for step in (x_state, y_state, x_rest, x_corner, y_middle, x_last, y_last):
        step[2]()


def hand_over(p_ref, m_ref, p_out, m_out, sem):
    copies = [pltpu.make_async_copy(p_ref, p_out, sem.at[0]), pltpu.make_async_copy(m_ref, m_out, sem.at[1])]
    for copy in copies:
        copy.start()
    for copy in copies:
        copy.wait()


def solution(mesh):
    nx_dev, ny_dev = mesh.shape["gx"], mesh.shape["gy"]
    split = P("gx", "gy", None)

    def on_device(*args):
        X, Y, Z = args[0].shape
        f32, i32 = jnp.float32, jnp.int32
        anywhere = pl.BlockSpec(memory_space=pl.ANY)
        scalars = pl.BlockSpec(memory_space=pltpu.SMEM)
        vmem = pltpu.VMEM
        copies = 2 * (2 + 2 + 5 + 2 + 4 + 2 + 2)
        results = pl.pallas_call(
            functools.partial(kernel, nx_dev, ny_dev),
            out_shape=[vmem((X, Y, Z), f32)] * 2,
            in_specs=[anywhere] * 7 + [scalars] * 2,
            out_specs=[pl.BlockSpec(memory_space=vmem)] * 2,
            scratch_shapes=(
                [vmem((X + 4, Y + 8, Z), f32)] * 2
                + [vmem((X + 2, Y, Z), f32)] * 2
                + [vmem((X + 2, Y, Z), i32)] * 3
                + [vmem((X + 2, Y + 8, Z), f32)] * 6
                + [vmem((X + 2, Y, Z), f32)] * 3
                + [vmem((X, Y, Z), f32)] * 4
                + [pltpu.SemaphoreType.DMA((7,))]
                + [pltpu.SemaphoreType.DMA((copies,))] * 2
            ),
            compiler_params=pltpu.CompilerParams(
                collective_id=0, has_side_effects=True, vmem_limit_bytes=32 * 1024 * 1024
            ),
            name="reverse",
        )(*args)
        return pl.pallas_call(
            hand_over,
            out_shape=[jax.ShapeDtypeStruct((X, Y, Z), f32)] * 2,
            in_specs=[pl.BlockSpec(memory_space=vmem)] * 2,
            out_specs=[anywhere] * 2,
            scratch_shapes=[pltpu.SemaphoreType.DMA((2,))],
            name="hand_over",
        )(*results)

    return jax.shard_map(
        on_device, mesh=mesh, in_specs=(split,) * 7 + (P(), P()), out_specs=(split, split), check_vma=False
    )
```

```python
import functools

import jax
import jax.numpy as jnp
from jax import lax
from jax.experimental import pallas as pl
from jax.experimental.pallas import tpu as pltpu
from jax.sharding import PartitionSpec as P

mobility_step = 0.1
well_height = 1.0
coupling = 1.0
diffusion_step = 0.03

MESH = pl.DeviceIdType.MESH


def pick(index, table, count):
    values = [table[k] for k in range(count)]
    bit = 1
    while len(values) > 1:
        odd = (index & bit) != 0
        values = [jnp.where(odd, values[k + 1], values[k]) for k in range(0, len(values), 2)]
        bit *= 2
    return values[0]


def local_terms(phase, jump):
    t = phase - phase * phase
    inverse = 1.0 / (1.0 - 2.0 * t)
    slope = 2.0 * t * inverse * inverse
    slope_derivative = 2.0 * (1.0 - 2.0 * phase) * (1.0 + 2.0 * t) * (inverse * inverse * inverse)
    release = 1.0 / (1.0 - jump * (phase * phase * inverse))
    return t, slope, slope_derivative, release


def kernel(
    nx_dev, ny_dev,
    p_hbm, m_hbm, a_hbm, b_hbm, or_hbm, an_hbm, bm_hbm, st_hbm, pt_hbm,
    out_p, out_m,
    P0, M0, A, B, OR, AN, BM, P1, M1, U1, V1, U0, V0,
    KAP, JMP, MOV, JS0, W0, G0, K0, st, pt,
    load_sem, ss, rs,
):
    X, Y, Z = p_hbm.shape
    HI, LO = Y, Y + 7
    gx, gy = lax.axis_index("gx"), lax.axis_index("gy")
    has = {
        ("x", 0): gx > 0, ("x", 1): gx < nx_dev - 1,
        ("y", 0): gy > 0, ("y", 1): gy < ny_dev - 1,
    }
    device = {
        ("x", 0): {"gx": gx - 1}, ("x", 1): {"gx": gx + 1},
        ("y", 0): {"gy": gy - 1}, ("y", 1): {"gy": gy + 1},
    }

    loads = []
    for k, (src, dst, off) in enumerate((
        (p_hbm, P0, 2), (m_hbm, M0, 2), (or_hbm, OR, 1), (an_hbm, AN, 1),
        (bm_hbm, BM, 1), (a_hbm, A, 1), (b_hbm, B, 1),
    )):
        copy = pltpu.make_async_copy(src, dst.at[pl.ds(off, X), pl.ds(0, Y), :], load_sem.at[k])
        copy.start()
        loads.append(copy)
    for k, (src, dst) in enumerate(((st_hbm, st), (pt_hbm, pt))):
        copy = pltpu.make_async_copy(src, dst, load_sem.at[7 + k])
        copy.start()
        loads.append(copy)

    barrier = pltpu.get_barrier_semaphore()
    count = jnp.int32(0)
    for key, there in has.items():
        @pl.when(there)
        def _():
            pl.semaphore_signal(barrier, inc=1, device_id=device[key], device_id_type=MESH)
        count = count + there.astype(jnp.int32)

    for side, (two, one) in enumerate(((0, 0), (X + 2, X + 1))):
        @pl.when(jnp.logical_not(has["x", side]))
        def _():
            for ref in (P0, M0):
                ref[pl.ds(two, 2)] = jnp.zeros((2,) + ref.shape[1:], ref.dtype)
            for ref in (A, B, OR, AN):
                ref[one] = jnp.zeros(ref.shape[1:], ref.dtype)
            BM[one] = jnp.ones(BM.shape[1:], BM.dtype)
            for ref in (U0, V0):
                ref[one] = jnp.zeros(ref.shape[1:], ref.dtype)
    for side, row in enumerate((LO, HI)):
        @pl.when(jnp.logical_not(has["y", side]))
        def _():
            for ref, off in ((P0, 2), (M0, 2), (P1, 1), (M1, 1), (U1, 1), (V1, 1), (U0, 1), (V0, 1)):
                ref[pl.ds(off, X), pl.ds(row, 1), :] = jnp.zeros((X, 1, Z), ref.dtype)

    sems = iter(range(ss.shape[0]))

    def exchange(axis, pieces):
        sends = {0: [], 1: []}
        arrivals = {0: [], 1: []}
        for ref, down, down_to, up, up_to in pieces:
            for side, src, dst in ((0, down, down_to), (1, up, up_to)):
                k = next(sems)
                copy = pltpu.make_async_remote_copy(
                    src_ref=ref.at[src], dst_ref=ref.at[dst], send_sem=ss.at[k], recv_sem=rs.at[k],
                    device_id=device[axis, side], device_id_type=MESH,
                )
                sends[side].append(copy)
                arrivals[1 - side].append(copy)

        def start():
            for side in (0, 1):
                @pl.when(has[axis, side])
                def _():
                    for copy in sends[side]:
                        copy.start()

        def wait_recv():
            for side in (0, 1):
                @pl.when(has[axis, side])
                def _():
                    for copy in arrivals[side]:
                        copy.wait_recv()

        def wait_send():
            for side in (0, 1):
                @pl.when(has[axis, side])
                def _():
                    for copy in sends[side]:
                        copy.wait_send()

        return start, wait_recv, wait_send

    rows = pl.ds(0, Y)

    def x_layers(ref, off, width):
        return (
            ref,
            (pl.ds(off, width), rows), (pl.ds(off + X, width), rows),
            (pl.ds(off + X - width, width), rows), (pl.ds(off - width, width), rows),
        )

    def y_rows(ref, off):
        own = pl.ds(off, X)
        return ref, (own, 0), (own, HI), (own, Y - 1), (own, LO)

    def corner(ref):
        tile = pl.ds(Y, 8)
        return ref, (2, tile), (X + 2, tile), (X + 1, tile), (1, tile)

    x_state = exchange("x", [x_layers(ref, 2, 2) for ref in (P0, M0)])
    y_state = exchange("y", [y_rows(ref, 2) for ref in (P0, M0)])
    x_rest = exchange("x", [x_layers(ref, 1, 1) for ref in (OR, AN, BM, A, B)])
    x_corner = exchange("x", [corner(ref) for ref in (P0, M0)])
    y_middle = exchange("y", [y_rows(ref, 1) for ref in (P1, M1, U1, V1)])
    x_last = exchange("x", [x_layers(ref, 1, 1) for ref in (U0, V0)])
    y_last = exchange("y", [y_rows(ref, 1) for ref in (U0, V0)])

    with jax.named_scope("wait_load"):
        loads[0].wait()
        loads[1].wait()
    with jax.named_scope("wait_barrier"):
        pl.semaphore_wait(barrier, count)
    with jax.named_scope("send_state"):
        x_state[0]()
        y_state[0]()
    with jax.named_scope("wait_load_rest"):
        for copy in loads[2:]:
            copy.wait()
    x_rest[0]()

    lane = lax.broadcasted_iota(jnp.int32, (Y, Z), 1)
    first, last = lane == 0, lane == Z - 1

    def lap(ref, i):
        wide = ref[i]
        center = wide[:Y]
        beside = ref[i - 1, :Y] + ref[i + 1, :Y]
        beside = beside + pltpu.roll(wide, Y + 7, 0)[:Y] + pltpu.roll(wide, 1, 0)[:Y]
        beside = beside + jnp.where(first, 0.0, pltpu.roll(center, 1, 1))
        beside = beside + jnp.where(last, 0.0, pltpu.roll(center, Z - 1, 1))
        return beside - 6.0 * center

    def tables(x):
        i = x + 1
        KAP[i] = pick(AN[i], st, st.shape[0])
        JMP[i] = 1.0 - pick(OR[i], pt, pt.shape[0])
        MOV[i] = 1.0 - BM[i].astype(jnp.float32)

    def forward(x, own):
        i = x + 1
        phase, potential = P0[x + 2, :Y], M0[x + 2, :Y]
        lap_phase, lap_potential = lap(P0, x + 2), lap(M0, x + 2)
        stiffness, jump, movable = KAP[i], JMP[i], MOV[i]
        t, slope, slope_derivative, release = local_terms(phase, jump)
        held_slope = jump * slope
        drive = (
            stiffness * lap_phase
            - 2.0 * well_height * t * (1.0 - 2.0 * phase)
            + coupling * held_slope * potential
        )
        step = movable * mobility_step * drive
        flux = (diffusion_step * lap_potential - held_slope * step) * release
        phase_next = phase + step
        potential_next = potential + movable * flux
        P1[i, :Y] = phase_next
        M1[i, :Y] = potential_next
        if own:
            JS0[x] = held_slope
            W0[x] = movable * release
            G0[x] = well_height * (12.0 * t - 2.0) + coupling * jump * slope_derivative * potential
            K0[x] = jump * (slope * flux - step * slope_derivative)
        _, slope, _, release = local_terms(phase_next, jump)
        spread = B[i] * (movable * release)
        pull = mobility_step * movable * (A[i] - spread * (jump * slope))
        U1[i, :Y] = stiffness * pull
        V1[i, :Y] = diffusion_step * spread

    def backward(x):
        i = x + 1
        phase, potential = P1[i, :Y], M1[i, :Y]
        stiffness, jump, movable = KAP[i], JMP[i], MOV[i]
        t, slope, slope_derivative, release = local_terms(phase, jump)
        held_slope = jump * slope
        drive = (
            stiffness * lap(P1, i)
            - 2.0 * well_height * t * (1.0 - 2.0 * phase)
            + coupling * held_slope * potential
        )
        step = movable * mobility_step * drive
        flux = (diffusion_step * lap(M1, i) - held_slope * step) * release
        gain = well_height * (12.0 * t - 2.0) + coupling * jump * slope_derivative * potential
        keep = jump * (slope * flux - step * slope_derivative)
        spread = B[i] * (movable * release)
        pull = mobility_step * movable * (A[i] - spread * held_slope)
        bar_p = A[i] + pull * gain + spread * keep + lap(U1, i)
        bar_m = B[i] + coupling * held_slope * pull + lap(V1, i)
        spread = bar_m * W0[x]
        pull = mobility_step * movable * (bar_p - spread * JS0[x])
        U0[i, :Y] = stiffness * pull
        V0[i, :Y] = diffusion_step * spread
        out_p[x] = bar_p + pull * G0[x] + spread * K0[x]
        out_m[x] = bar_m + coupling * JS0[x] * pull

    def finish(x):
        out_p[x] = out_p[x] + lap(U0, x + 1)
        out_m[x] = out_m[x] + lap(V0, x + 1)

    def over(low, high, body):
        def step(x, carry):
            body(x)
            return carry
        lax.fori_loop(low, high, step, 0)

    with jax.named_scope("tables"):
        over(0, X, tables)
    with jax.named_scope("wait_y_state"):
        y_state[1]()
    x_corner[0]()
    with jax.named_scope("forward_inside"):
        over(1, X - 1, lambda x: forward(x, True))
    with jax.named_scope("wait_x_state"):
        x_state[1]()
    with jax.named_scope("forward_edge"):
        over(0, 2, lambda k: forward(k * (X - 1), True))
        y_middle[0]()
    with jax.named_scope("wait_x_rest"):
        x_rest[1]()
    with jax.named_scope("wait_x_corner"):
        x_corner[1]()
    with jax.named_scope("forward_halo"):
        over(0, 2, lambda k: tables(k * (X + 1) - 1))
        over(0, 2, lambda k: forward(k * (X + 1) - 1, False))
    with jax.named_scope("wait_y_middle"):
        y_middle[1]()
    with jax.named_scope("backward_edge"):
        over(0, 2, lambda k: backward(k * (X - 1)))
        x_last[0]()
    with jax.named_scope("backward_inside"):
        over(1, X - 1, backward)
        y_last[0]()
    with jax.named_scope("wait_y_last"):
        y_last[1]()
    with jax.named_scope("finish_inside"):
        over(1, X - 1, finish)
    with jax.named_scope("wait_x_last"):
        x_last[1]()
    with jax.named_scope("finish_edge"):
        over(0, 2, lambda k: finish(k * (X - 1)))
    with jax.named_scope("wait_sends"):
        for step in (x_state, y_state, x_rest, x_corner, y_middle, x_last, y_last):
            step[2]()


def hand_over(p_ref, m_ref, p_out, m_out, sem):
    copies = [pltpu.make_async_copy(p_ref, p_out, sem.at[0]), pltpu.make_async_copy(m_ref, m_out, sem.at[1])]
    for copy in copies:
        copy.start()
    for copy in copies:
        copy.wait()


def solution(mesh):
    nx_dev, ny_dev = mesh.shape["gx"], mesh.shape["gy"]
    split = P("gx", "gy", None)

    def on_device(*args):
        X, Y, Z = args[0].shape
        f32, i32 = jnp.float32, jnp.int32
        hbm = pl.BlockSpec(memory_space=pltpu.HBM)
        vmem = pltpu.VMEM
        copies = 2 * (2 + 2 + 5 + 2 + 4 + 2 + 2)
        results = pl.pallas_call(
            functools.partial(kernel, nx_dev, ny_dev),
            out_shape=[vmem((X, Y, Z), f32)] * 2,
            in_specs=[hbm] * 9,
            out_specs=[pl.BlockSpec(memory_space=vmem)] * 2,
            scratch_shapes=(
                [vmem((X + 4, Y + 8, Z), f32)] * 2
                + [vmem((X + 2, Y, Z), f32)] * 2
                + [vmem((X + 2, Y, Z), i32)] * 3
                + [vmem((X + 2, Y + 8, Z), f32)] * 6
                + [vmem((X + 2, Y, Z), f32)] * 3
                + [vmem((X, Y, Z), f32)] * 4
                + [pltpu.SMEM(args[7].shape, f32), pltpu.SMEM(args[8].shape, f32)]
                + [pltpu.SemaphoreType.DMA((9,))]
                + [pltpu.SemaphoreType.DMA((copies,))] * 2
            ),
            compiler_params=pltpu.CompilerParams(
                collective_id=0, has_side_effects=True, vmem_limit_bytes=32 * 1024 * 1024
            ),
            name="reverse",
        )(*[pltpu.with_memory_space_constraint(arg, pltpu.HBM) for arg in args])
        results = [pltpu.with_memory_space_constraint(r, vmem) for r in results]
        return pl.pallas_call(
            hand_over,
            out_shape=[jax.ShapeDtypeStruct((X, Y, Z), f32)] * 2,
            in_specs=[pl.BlockSpec(memory_space=vmem)] * 2,
            out_specs=[hbm] * 2,
            scratch_shapes=[pltpu.SemaphoreType.DMA((2,))],
            name="hand_over",
        )(*results)

    return jax.shard_map(
        on_device, mesh=mesh, in_specs=(split,) * 7 + (P(), P()), out_specs=(split, split), check_vma=False
    )
```

```python
import functools

import jax
import jax.numpy as jnp
from jax import lax
from jax.experimental import pallas as pl
from jax.experimental.pallas import tpu as pltpu
from jax.sharding import PartitionSpec as P

mobility_step = 0.1
well_height = 1.0
coupling = 1.0
diffusion_step = 0.03

MESH = pl.DeviceIdType.MESH


def pick(index, table, count):
    values = [table[k] for k in range(count)]
    bit = 1
    while len(values) > 1:
        odd = (index & bit) != 0
        values = [jnp.where(odd, values[k + 1], values[k]) for k in range(0, len(values), 2)]
        bit *= 2
    return values[0]


def local_terms(phase, jump):
    t = phase - phase * phase
    inverse = 1.0 / (1.0 - 2.0 * t)
    slope = 2.0 * t * inverse * inverse
    slope_derivative = 2.0 * (1.0 - 2.0 * phase) * (1.0 + 2.0 * t) * (inverse * inverse * inverse)
    release = 1.0 / (1.0 - jump * (phase * phase * inverse))
    return t, slope, slope_derivative, release


def kernel(
    nx_dev, ny_dev,
    p_hbm, m_hbm, a_hbm, b_hbm, or_hbm, an_hbm, bm_hbm, st_hbm, pt_hbm,
    out_p, out_m,
    A, B, OR, AN, BM, P0, M0, P1, M1, U1, V1, U0, V0, UD, VD, UU, VU,
    KAP, JMP, MOV, JS0, W0, G0, K0, st, pt,
    load_sem, ss, rs,
):
    X, Y, Z = p_hbm.shape
    HI, LO = Y, Y + 7
    gx, gy = lax.axis_index("gx"), lax.axis_index("gy")
    has = {
        ("x", 0): gx > 0, ("x", 1): gx < nx_dev - 1,
        ("y", 0): gy > 0, ("y", 1): gy < ny_dev - 1,
    }
    device = {
        ("x", 0): {"gx": gx - 1}, ("x", 1): {"gx": gx + 1},
        ("y", 0): {"gy": gy - 1}, ("y", 1): {"gy": gy + 1},
    }

    barrier = pltpu.get_barrier_semaphore()
    count = jnp.int32(0)
    for key, there in has.items():
        @pl.when(there)
        def _():
            pl.semaphore_signal(barrier, inc=1, device_id=device[key], device_id_type=MESH)
        count = count + there.astype(jnp.int32)

    rows = pl.ds(0, Y)
    loads = []
    for k, (src, dst) in enumerate((
        (p_hbm, P0.at[pl.ds(1, X), rows]), (m_hbm, M0.at[pl.ds(1, X), rows]),
        (an_hbm, AN), (or_hbm, OR), (bm_hbm, BM), (st_hbm, st), (pt_hbm, pt), (a_hbm, A), (b_hbm, B),
    )):
        copy = pltpu.make_async_copy(src, dst, load_sem.at[k])
        copy.start()
        loads.append(copy)

    sems = iter(range(ss.shape[0]))

    def exchange(axis, pieces):
        sends = {0: [], 1: []}
        arrivals = {0: [], 1: []}
        for down, down_to, up, up_to in pieces:
            for side, src, dst in ((0, down, down_to), (1, up, up_to)):
                k = next(sems)
                copy = pltpu.make_async_remote_copy(
                    src_ref=src, dst_ref=dst, send_sem=ss.at[k], recv_sem=rs.at[k],
                    device_id=device[axis, side], device_id_type=MESH,
                )
                sends[side].append(copy)
                arrivals[1 - side].append(copy)

        def each(groups, act):
            def run(sides=(0, 1)):
                for side in sides:
                    @pl.when(has[axis, side])
                    def _():
                        for copy in groups[side]:
                            act(copy)
            return run

        return (
            each(sends, lambda copy: copy.start()),
            each(arrivals, lambda copy: copy.wait_recv()),
            each(sends, lambda copy: copy.wait_send()),
        )

    def x_faces(ref):
        return ref.at[1, rows], ref.at[X + 1, rows], ref.at[X, rows], ref.at[0, rows]

    def y_faces(ref):
        own = pl.ds(1, X)
        return ref.at[own, 0], ref.at[own, HI], ref.at[own, Y - 1], ref.at[own, LO]

    def y_aside(ref, up, down):
        own = pl.ds(1, X)
        return ref.at[own, 0], up.at[:, 0], ref.at[own, Y - 1], down.at[:, 0]

    x_state = exchange("x", [
        (src.at[0], dst.at[X + 1, rows], src.at[X - 1], dst.at[0, rows]) for src, dst in ((p_hbm, P0), (m_hbm, M0))
    ])
    y_state = exchange("y", [y_faces(ref) for ref in (P0, M0)])
    x_middle = exchange("x", [x_faces(ref) for ref in (P1, M1, U1, V1)])
    y_middle = exchange("y", [y_faces(ref) for ref in (P1, M1, U1, V1)])
    x_last = exchange("x", [x_faces(ref) for ref in (U0, V0)])
    y_last = exchange("y", [y_aside(U0, UU, UD), y_aside(V0, VU, VD)])

    for side, layer in enumerate((0, X + 1)):
        @pl.when(jnp.logical_not(has["x", side]))
        def _():
            for ref in (P0, M0, P1, M1, U1, V1, U0, V0):
                ref[layer, :Y] = jnp.zeros((Y, Z), ref.dtype)
    for side, (row, aside) in enumerate(((LO, (UD, VD)), (HI, (UU, VU)))):
        @pl.when(jnp.logical_not(has["y", side]))
        def _():
            for ref in (P0, M0, P1, M1, U1, V1):
                ref[pl.ds(1, X), pl.ds(row, 1), :] = jnp.zeros((X, 1, Z), ref.dtype)
            for ref in aside:
                ref[:, pl.ds(0, 1), :] = jnp.zeros((X, 1, Z), ref.dtype)
    for ref in (U0, V0):
        ref[:, Y:, :] = jnp.zeros((X + 2, 8, Z), ref.dtype)

    with jax.named_scope("wait_barrier"):
        pl.semaphore_wait(barrier, count)
    x_state[0]()
    with jax.named_scope("wait_load"):
        loads[0].wait()
        loads[1].wait()
    y_state[0]()
    with jax.named_scope("wait_load_rest"):
        for copy in loads[2:]:
            copy.wait()

    lane = lax.broadcasted_iota(jnp.int32, (Y, Z), 1)
    first, last = lane == 0, lane == Z - 1

    def lap(ref, i, below=True, above=True):
        wide = ref[i]
        center = wide[:Y]
        beside = pltpu.roll(wide, Y + 7, 0)[:Y] + pltpu.roll(wide, 1, 0)[:Y]
        if below:
            beside = beside + ref[i - 1, :Y]
        if above:
            beside = beside + ref[i + 1, :Y]
        beside = beside + jnp.where(first, 0.0, pltpu.roll(center, 1, 1))
        beside = beside + jnp.where(last, 0.0, pltpu.roll(center, Z - 1, 1))
        return beside - 6.0 * center

    def tables(x):
        KAP[x] = pick(AN[x], st, st.shape[0])
        JMP[x] = 1.0 - pick(OR[x], pt, pt.shape[0])
        MOV[x] = 1.0 - BM[x].astype(jnp.float32)

    def forward(x):
        i = x + 1
        phase, potential = P0[i, :Y], M0[i, :Y]
        stiffness, jump, movable = KAP[x], JMP[x], MOV[x]
        t, slope, slope_derivative, release = local_terms(phase, jump)
        held_slope = jump * slope
        drive = (
            stiffness * lap(P0, i)
            - 2.0 * well_height * t * (1.0 - 2.0 * phase)
            + coupling * held_slope * potential
        )
        step = movable * mobility_step * drive
        flux = (diffusion_step * lap(M0, i) - held_slope * step) * release
        phase_next = phase + step
        P1[i, :Y] = phase_next
        M1[i, :Y] = potential + movable * flux
        JS0[x] = held_slope
        W0[x] = movable * release
        G0[x] = well_height * (12.0 * t - 2.0) + coupling * jump * slope_derivative * potential
        K0[x] = jump * (slope * flux - step * slope_derivative)
        _, slope, _, release = local_terms(phase_next, jump)
        spread = B[x] * (movable * release)
        pull = mobility_step * movable * (A[x] - spread * (jump * slope))
        U1[i, :Y] = stiffness * pull
        V1[i, :Y] = diffusion_step * spread

    def backward(x):
        i = x + 1
        phase, potential = P1[i, :Y], M1[i, :Y]
        stiffness, jump, movable = KAP[x], JMP[x], MOV[x]
        t, slope, slope_derivative, release = local_terms(phase, jump)
        held_slope = jump * slope
        drive = (
            stiffness * lap(P1, i)
            - 2.0 * well_height * t * (1.0 - 2.0 * phase)
            + coupling * held_slope * potential
        )
        step = movable * mobility_step * drive
        flux = (diffusion_step * lap(M1, i) - held_slope * step) * release
        gain = well_height * (12.0 * t - 2.0) + coupling * jump * slope_derivative * potential
        keep = jump * (slope * flux - step * slope_derivative)
        spread = B[x] * (movable * release)
        pull = mobility_step * movable * (A[x] - spread * held_slope)
        bar_p = A[x] + pull * gain + spread * keep + lap(U1, i)
        bar_m = B[x] + coupling * held_slope * pull + lap(V1, i)
        spread = bar_m * W0[x]
        pull = mobility_step * movable * (bar_p - spread * JS0[x])
        U0[i, :Y] = stiffness * pull
        V0[i, :Y] = diffusion_step * spread
        out_p[x] = bar_p + pull * G0[x] + spread * K0[x]
        out_m[x] = bar_m + coupling * JS0[x] * pull

    def finish(x, **sides):
        out_p[x] = out_p[x] + lap(U0, x + 1, **sides)
        out_m[x] = out_m[x] + lap(V0, x + 1, **sides)

    def finish_rows(x):
        for out, down, up in ((out_p, UD, UU), (out_m, VD, VU)):
            out[x, 0:1] = out[x, 0:1] + down[x, 0:1]
            out[x, Y - 1:Y] = out[x, Y - 1:Y] + up[x, 0:1]

    def over(low, high, body):
        def step(x, carry):
            body(x)
            return carry
        lax.fori_loop(low, high, step, 0, unroll=2)

    def edges(body):
        over(0, 2, lambda k: body(k * (X - 1)))

    with jax.named_scope("tables"):
        over(0, X, tables)
    with jax.named_scope("wait_y_state"):
        y_state[1]()
    with jax.named_scope("forward_inside"):
        over(1, X - 1, forward)
    with jax.named_scope("wait_x_state"):
        x_state[1]()
    with jax.named_scope("forward_edge"):
        edges(forward)
        x_middle[0]()
        y_middle[0]()
    with jax.named_scope("wait_middle"):
        y_middle[1]()
        x_middle[1]()
    with jax.named_scope("backward_edge"):
        edges(backward)
        x_last[0]()
    with jax.named_scope("backward_inside"):
        over(1, X - 1, backward)
        y_last[0]()
    with jax.named_scope("finish_inside"):
        over(1, X - 1, finish)
        finish(0, below=False)
        finish(X - 1, above=False)
    with jax.named_scope("wait_y_last"):
        y_last[1]()
        over(0, X, finish_rows)
    with jax.named_scope("wait_x_last"):
        x_last[1]()
        for x, layer in ((0, 0), (X - 1, X + 1)):
            out_p[x] = out_p[x] + U0[layer, :Y]
            out_m[x] = out_m[x] + V0[layer, :Y]
    with jax.named_scope("wait_sends"):
        for step in (x_state, y_state, x_middle, y_middle, x_last, y_last):
            step[2]()


def hand_over(p_ref, m_ref, p_out, m_out, sem):
    copies = [pltpu.make_async_copy(p_ref, p_out, sem.at[0]), pltpu.make_async_copy(m_ref, m_out, sem.at[1])]
    for copy in copies:
        copy.start()
    for copy in copies:
        copy.wait()


def solution(mesh):
    nx_dev, ny_dev = mesh.shape["gx"], mesh.shape["gy"]
    split = P("gx", "gy", None)

    def on_device(*args):
        X, Y, Z = args[0].shape
        f32, i32 = jnp.float32, jnp.int32
        hbm = pl.BlockSpec(memory_space=pltpu.HBM)
        vmem = pltpu.VMEM
        copies = 2 * 2 * (2 + 4 + 2)
        results = pl.pallas_call(
            functools.partial(kernel, nx_dev, ny_dev),
            out_shape=[vmem((X, Y, Z), f32)] * 2,
            in_specs=[hbm] * 9,
            out_specs=[pl.BlockSpec(memory_space=vmem)] * 2,
            scratch_shapes=(
                [vmem((X, Y, Z), f32)] * 2
                + [vmem((X, Y, Z), i32)] * 3
                + [vmem((X + 2, Y + 8, Z), f32)] * 8
                + [vmem((X, 8, Z), f32)] * 4
                + [vmem((X, Y, Z), f32)] * 7
                + [pltpu.SMEM(args[7].shape, f32), pltpu.SMEM(args[8].shape, f32)]
                + [pltpu.SemaphoreType.DMA((9,))]
                + [pltpu.SemaphoreType.DMA((copies,))] * 2
            ),
            compiler_params=pltpu.CompilerParams(
                collective_id=0, has_side_effects=True, vmem_limit_bytes=32 * 1024 * 1024
            ),
            name="reverse",
        )(*[pltpu.with_memory_space_constraint(arg, pltpu.HBM) for arg in args])
        results = [pltpu.with_memory_space_constraint(r, vmem) for r in results]
        return pl.pallas_call(
            hand_over,
            out_shape=[jax.ShapeDtypeStruct((X, Y, Z), f32)] * 2,
            in_specs=[pl.BlockSpec(memory_space=vmem)] * 2,
            out_specs=[hbm] * 2,
            scratch_shapes=[pltpu.SemaphoreType.DMA((2,))],
            name="hand_over",
        )(*results)

    return jax.shard_map(
        on_device, mesh=mesh, in_specs=(split,) * 7 + (P(), P()), out_specs=(split, split), check_vma=False
    )
```

```python
import functools

import jax
import jax.numpy as jnp
from jax import lax
from jax.experimental import pallas as pl
from jax.experimental.pallas import tpu as pltpu
from jax.sharding import PartitionSpec as P

mobility_step = 0.1
well_height = 1.0
coupling = 1.0
diffusion_step = 0.03

MESH = pl.DeviceIdType.MESH


def pick(index, table, count):
    values = [table[k] for k in range(count)]
    bit = 1
    while len(values) > 1:
        odd = (index & bit) != 0
        values = [jnp.where(odd, values[k + 1], values[k]) for k in range(0, len(values), 2)]
        bit *= 2
    return values[0]


def local_terms(phase, jump):
    t = phase - phase * phase
    denominator = 1.0 - 2.0 * t
    rest = denominator - jump * (phase - t)
    both = 1.0 / (denominator * rest)
    inverse = rest * both
    release = denominator * (denominator * both)
    square = inverse * inverse
    slope = 2.0 * t * square
    slope_derivative = (2.0 - 4.0 * phase) * (1.0 + 2.0 * t) * (square * inverse)
    return t, slope, slope_derivative, release


def kernel(
    nx_dev, ny_dev,
    p_hbm, m_hbm, a_hbm, b_hbm, or_hbm, an_hbm, bm_hbm, st_hbm, pt_hbm,
    out_p, out_m,
    A, B, OR, AN, BM, P0, M0, P1, M1, U1, V1, U0, V0, HP0, HM0, HP1, HM1, HU1, HV1, HU0, HV0,
    KAP, JMP, MOV, REACH, JS0, JD0, W0, G0, K0, JS1, JD1, W1, SP1, st, pt,
    load_sem, ss, rs,
):
    X, Y, Z = p_hbm.shape
    gx, gy = lax.axis_index("gx"), lax.axis_index("gy")
    has = {
        ("x", 0): gx > 0, ("x", 1): gx < nx_dev - 1,
        ("y", 0): gy > 0, ("y", 1): gy < ny_dev - 1,
    }
    device = {
        ("x", 0): {"gx": gx - 1}, ("x", 1): {"gx": gx + 1},
        ("y", 0): {"gy": gy - 1}, ("y", 1): {"gy": gy + 1},
    }

    barrier = pltpu.get_barrier_semaphore()
    count = jnp.int32(0)
    for key, there in has.items():
        @pl.when(there)
        def _():
            pl.semaphore_signal(barrier, inc=1, device_id=device[key], device_id_type=MESH)
        count = count + there.astype(jnp.int32)

    own = pl.ds(1, X)
    loads = []
    for k, (src, dst) in enumerate((
        (p_hbm, P0.at[own]), (m_hbm, M0.at[own]),
        (an_hbm, AN.at[own]), (or_hbm, OR.at[own]), (bm_hbm, BM.at[own]), (st_hbm, st), (pt_hbm, pt),
        (a_hbm, A.at[own]), (b_hbm, B.at[own]),
    )):
        copy = pltpu.make_async_copy(src, dst, load_sem.at[k])
        copy.start()
        loads.append(copy)

    sems = iter(range(ss.shape[0]))

    def exchange(axis, pieces):
        sends = {0: [], 1: []}
        arrivals = {0: [], 1: []}
        for down, down_to, up, up_to in pieces:
            for side, src, dst in ((0, down, down_to), (1, up, up_to)):
                k = next(sems)
                copy = pltpu.make_async_remote_copy(
                    src_ref=src, dst_ref=dst, send_sem=ss.at[k], recv_sem=rs.at[k],
                    device_id=device[axis, side], device_id_type=MESH,
                )
                sends[side].append(copy)
                arrivals[1 - side].append(copy)

        def each(groups, act):
            def run(sides=(0, 1)):
                for side in sides:
                    @pl.when(has[axis, side])
                    def _():
                        for copy in groups[side]:
                            act(copy)
            return run

        return (
            each(sends, lambda copy: copy.start()),
            each(arrivals, lambda copy: copy.wait_recv()),
            each(sends, lambda copy: copy.wait_send()),
        )

    def x_faces(ref):
        return ref.at[1], ref.at[X + 1], ref.at[X], ref.at[0]

    def y_faces(ref, aside):
        return ref.at[own, 0], aside.at[:, 7], ref.at[own, Y - 1], aside.at[:, 0]

    def x_given(src, dst):
        return src.at[0], dst.at[X + 1], src.at[X - 1], dst.at[0]

    x_state = exchange("x", [x_faces(P0), x_faces(M0)])
    x_given_rest = exchange("x", [
        x_given(src, dst) for src, dst in ((an_hbm, AN), (or_hbm, OR), (bm_hbm, BM), (a_hbm, A), (b_hbm, B))
    ])
    y_state = exchange("y", [y_faces(P0, HP0), y_faces(M0, HM0)])
    x_middle = exchange("x", [x_faces(ref) for ref in (P1, M1)])
    y_middle = exchange("y", [y_faces(P1, HP1), y_faces(M1, HM1), y_faces(U1, HU1), y_faces(V1, HV1)])
    x_last = exchange("x", [x_faces(ref) for ref in (U0, V0)])
    y_last = exchange("y", [y_faces(U0, HU0), y_faces(V0, HV0)])

    for side, layer in enumerate((0, X + 1)):
        @pl.when(jnp.logical_not(has["x", side]))
        def _():
            for ref in (P0, M0, P1, M1, U1, V1, U0, V0):
                ref[layer] = jnp.zeros((Y, Z), ref.dtype)

    with jax.named_scope("wait_barrier"):
        pl.semaphore_wait(barrier, count)
    pass
    with jax.named_scope("wait_load"):
        loads[0].wait()
        loads[1].wait()
    x_state[0]()
    y_state[0]()
    x_given_rest[0]()
    with jax.named_scope("wait_load_rest"):
        for copy in loads[2:]:
            copy.wait()

    lane = lax.broadcasted_iota(jnp.int32, (8, 128), 1)
    line = lax.broadcasted_iota(jnp.int32, (8, 128), 0)
    first_lane, last_lane, first_line, last_line = lane == 0, lane == 127, line == 0, line == 7

    def shifted(parts, by, size, axis, edge):
        turned = [pltpu.roll(part, by % size, axis) for part in parts]
        return [jnp.where(edge, before, here) for before, here in zip([0.0] + turned, turned)]

    def lap(ref, i, below=True, above=True):
        tiles = [[ref[i, a:a + 8, b:b + 128] for b in range(0, Z, 128)] for a in range(0, Y, 8)]
        result = []
        along_y = []
        for column in zip(*tiles):
            down = shifted(column, 1, 8, 0, first_line)
            up = shifted(column[::-1], -1, 8, 0, last_line)[::-1]
            along_y.append([d + u for d, u in zip(down, up)])
        for a, row in enumerate(tiles):
            left = shifted(row, 1, 128, 1, first_lane)
            right = shifted(row[::-1], -1, 128, 1, last_lane)[::-1]
            result.append(jnp.concatenate(
                [l + r + along_y[b][a] - 6.0 * c for b, (l, r, c) in enumerate(zip(left, right, row))], axis=1
            ))
        beside = jnp.concatenate(result, axis=0)
        if below:
            beside = beside + ref[i - 1]
        if above:
            beside = beside + ref[i + 1]
        return beside

    def tables(i):
        KAP[i] = pick(AN[i], st, st.shape[0])
        JMP[i] = 1.0 - pick(OR[i], pt, pt.shape[0])
        movable = 1.0 - BM[i].astype(jnp.float32)
        MOV[i] = movable
        REACH[i] = mobility_step * movable

    def sensitivities(at, phase):
        jump = JMP[at]
        _, slope, _, release = local_terms(phase, jump)
        spread = B[at] * (MOV[at] * release)
        U1[at] = KAP[at] * (REACH[at] * (A[at] - spread * (jump * slope)))
        V1[at] = diffusion_step * spread

    def forward(x):
        i = x + 1
        phase, potential = P0[i], M0[i]
        jump = JMP[i]
        t, slope, slope_derivative, release = local_terms(phase, jump)
        held_slope, held_derivative = jump * slope, jump * slope_derivative
        drive = (
            KAP[i] * lap(P0, i)
            - 2.0 * well_height * t * (1.0 - 2.0 * phase)
            + coupling * held_slope * potential
        )
        step = REACH[i] * drive
        yielding = MOV[i] * release
        flux = yielding * (diffusion_step * lap(M0, i) - held_slope * step)
        P1[i] = phase + step
        M1[i] = potential + flux
        JS0[x] = held_slope
        JD0[x] = held_derivative
        W0[x] = yielding
        G0[x] = well_height * (12.0 * t - 2.0) + coupling * held_derivative * potential
        K0[x] = held_slope * flux - held_derivative * step
        sensitivities(i, phase + step)

    def forward_row(x, row, aside):
        at, here, away = (x, slice(row, row + 1)), (x + 1, slice(row, row + 1)), (x, slice(aside, aside + 1))
        step = REACH[here] * KAP[here] * HP0[away]
        flux = W0[at] * (diffusion_step * HM0[away] - JS0[at] * step)
        phase = P1[here] + step
        P1[here] = phase
        M1[here] = M1[here] + flux
        K0[at] = K0[at] + JS0[at] * flux - JD0[at] * step
        sensitivities(here, phase)

    def backward(x):
        i = x + 1
        phase, potential = P1[i], M1[i]
        jump, reach = JMP[i], REACH[i]
        t, slope, slope_derivative, release = local_terms(phase, jump)
        held_slope, held_derivative = jump * slope, jump * slope_derivative
        drive = (
            KAP[i] * lap(P1, i)
            - 2.0 * well_height * t * (1.0 - 2.0 * phase)
            + coupling * held_slope * potential
        )
        step = reach * drive
        yielding = MOV[i] * release
        flux = yielding * (diffusion_step * lap(M1, i) - held_slope * step)
        gain = well_height * (12.0 * t - 2.0) + coupling * held_derivative * potential
        keep = held_slope * flux - held_derivative * step
        spread = B[i] * yielding
        pull = reach * (A[i] - spread * held_slope)
        JS1[x] = held_slope
        JD1[x] = held_derivative
        W1[x] = yielding
        SP1[x] = spread
        bar_p = A[i] + pull * gain + spread * keep + lap(U1, i)
        bar_m = B[i] + coupling * held_slope * pull + lap(V1, i)
        spread = bar_m * W0[x]
        pull = reach * (bar_p - spread * JS0[x])
        U0[i] = KAP[i] * pull
        V0[i] = diffusion_step * spread
        out_p[x] = bar_p + pull * G0[x] + spread * K0[x]
        out_m[x] = bar_m + coupling * JS0[x] * pull

    def backward_row(x, row, aside):
        at, here, away = (x, slice(row, row + 1)), (x + 1, slice(row, row + 1)), (x, slice(aside, aside + 1))
        step = REACH[here] * KAP[here] * HP1[away]
        flux = W1[at] * (diffusion_step * HM1[away] - JS1[at] * step)
        bar_p = SP1[at] * (JS1[at] * flux - JD1[at] * step) + HU1[away]
        bar_m = HV1[away]
        spread = bar_m * W0[at]
        pull = REACH[here] * (bar_p - spread * JS0[at])
        U0[here] = U0[here] + KAP[here] * pull
        V0[here] = V0[here] + diffusion_step * spread
        out_p[at] = out_p[at] + (bar_p + pull * G0[at] + spread * K0[at])
        out_m[at] = out_m[at] + (bar_m + coupling * JS0[at] * pull)

    def finish(x, **sides):
        out_p[x] = out_p[x] + lap(U0, x + 1, **sides)
        out_m[x] = out_m[x] + lap(V0, x + 1, **sides)

    def finish_row(x, row, aside):
        at, away = (x, slice(row, row + 1)), (x, slice(aside, aside + 1))
        out_p[at] = out_p[at] + HU0[away]
        out_m[at] = out_m[at] + HV0[away]

    def over(low, high, body, unroll=2):
        def step(x, carry):
            body(x)
            return carry
        lax.fori_loop(low, high, step, 0, unroll=unroll)

    def edges(body):
        over(0, 2, lambda k: body(k * (X - 1)))

    def by_rows(run, body):
        for side, row, aside in ((0, 0, 0), (1, Y - 1, 7)):
            @pl.when(has["y", side])
            def _():
                run(lambda x: body(x, row, aside))

    def inside_rows(body):
        by_rows(lambda act: over(1, X - 1, act, 2), body)

    def edge_rows(body):
        by_rows(edges, body)

    with jax.named_scope("tables"):
        over(1, X + 1, tables)
    with jax.named_scope("forward_inside"):
        over(1, X - 1, forward)
    with jax.named_scope("forward_edges"):
        y_state[1]()
        x_state[1]()
        edges(forward)
        edge_rows(forward_row)
        x_middle[0]()
    with jax.named_scope("forward_rows"):
        inside_rows(forward_row)
        y_middle[0]()
    with jax.named_scope("backward_inside"):
        x_given_rest[1]()
        over(0, 2, lambda k: tables(k * (X + 1)))
        over(1, X - 1, backward)
    with jax.named_scope("backward_edges"):
        y_middle[1]()
        x_middle[1]()
        for side, layer in enumerate((0, X + 1)):
            @pl.when(has["x", side])
            def _():
                sensitivities(layer, P1[layer])
        edges(backward)
        edge_rows(backward_row)
        x_last[0]()
    with jax.named_scope("backward_rows"):
        inside_rows(backward_row)
        y_last[0]()
    with jax.named_scope("finish_inside"):
        over(1, X - 1, finish)
        finish(0, below=False)
        finish(X - 1, above=False)
    with jax.named_scope("finish_rows"):
        y_last[1]()
        by_rows(lambda act: over(0, X, act, 4), finish_row)
    with jax.named_scope("finish_edges"):
        x_last[1]()
        for x, layer in ((0, 0), (X - 1, X + 1)):
            out_p[x] = out_p[x] + U0[layer]
            out_m[x] = out_m[x] + V0[layer]
    with jax.named_scope("wait_sends"):
        for step in (x_state, y_state, x_given_rest, x_middle, y_middle, x_last, y_last):
            step[2]()


def hand_over(p_ref, m_ref, p_out, m_out, sem):
    copies = [pltpu.make_async_copy(p_ref, p_out, sem.at[0]), pltpu.make_async_copy(m_ref, m_out, sem.at[1])]
    for copy in copies:
        copy.start()
    for copy in copies:
        copy.wait()


def solution(mesh):
    nx_dev, ny_dev = mesh.shape["gx"], mesh.shape["gy"]
    split = P("gx", "gy", None)

    def on_device(*args):
        X, Y, Z = args[0].shape
        f32, i32 = jnp.float32, jnp.int32
        hbm = pl.BlockSpec(memory_space=pltpu.HBM)
        vmem = pltpu.VMEM
        copies = 2 * (2 + 5 + 2 + 2) + 2 * (2 + 4 + 2)
        results = pl.pallas_call(
            functools.partial(kernel, nx_dev, ny_dev),
            out_shape=[vmem((X, Y, Z), f32)] * 2,
            in_specs=[hbm] * 9,
            out_specs=[pl.BlockSpec(memory_space=vmem)] * 2,
            scratch_shapes=(
                [vmem((X + 2, Y, Z), f32)] * 2
                + [vmem((X + 2, Y, Z), i32)] * 3
                + [vmem((X + 2, Y, Z), f32)] * 8
                + [vmem((X, 8, Z), f32)] * 8
                + [vmem((X + 2, Y, Z), f32)] * 4
                + [vmem((X, Y, Z), f32)] * 9
                + [pltpu.SMEM(args[7].shape, f32), pltpu.SMEM(args[8].shape, f32)]
                + [pltpu.SemaphoreType.DMA((9,))]
                + [pltpu.SemaphoreType.DMA((copies,))] * 2
            ),
            compiler_params=pltpu.CompilerParams(
                collective_id=0, has_side_effects=True, vmem_limit_bytes=32 * 1024 * 1024
            ),
            name="reverse",
        )(*[pltpu.with_memory_space_constraint(arg, pltpu.HBM) for arg in args])
        results = [pltpu.with_memory_space_constraint(r, vmem) for r in results]
        return pl.pallas_call(
            hand_over,
            out_shape=[jax.ShapeDtypeStruct((X, Y, Z), f32)] * 2,
            in_specs=[pl.BlockSpec(memory_space=vmem)] * 2,
            out_specs=[hbm] * 2,
            scratch_shapes=[pltpu.SemaphoreType.DMA((2,))],
            name="hand_over",
        )(*results)

    return jax.shard_map(
        on_device, mesh=mesh, in_specs=(split,) * 7 + (P(), P()), out_specs=(split, split), check_vma=False
    )
```

```python
import functools

import jax
import jax.numpy as jnp
from jax import lax
from jax.experimental import pallas as pl
from jax.experimental.pallas import tpu as pltpu
from jax.sharding import PartitionSpec as P

mobility_step = 0.1
well_height = 1.0
coupling = 1.0
diffusion_step = 0.03

MESH = pl.DeviceIdType.MESH


def pick(index, table, count):
    values = [table[k] for k in range(count)]
    bit = 1
    while len(values) > 1:
        odd = (index & bit) != 0
        values = [jnp.where(odd, values[k + 1], values[k]) for k in range(0, len(values), 2)]
        bit *= 2
    return values[0]


def local_terms(phase, jump):
    t = phase - phase * phase
    denominator = 1.0 - 2.0 * t
    rest = denominator - jump * (phase - t)
    both = 1.0 / (denominator * rest)
    inverse = rest * both
    release = denominator * (denominator * both)
    square = inverse * inverse
    slope = 2.0 * t * square
    slope_derivative = (2.0 - 4.0 * phase) * (1.0 + 2.0 * t) * (square * inverse)
    return t, slope, slope_derivative, release


def kernel(
    nx_dev, ny_dev,
    p_hbm, m_hbm, a_hbm, b_hbm, or_hbm, an_hbm, bm_hbm, st_hbm, pt_hbm,
    out_p, out_m,
    A, B, OR, AN, BM, P0, M0, P1, M1, U1, V1, U0, V0, CO, CI, HP0, HM0, HP1, HM1, HU1, HV1, HU0, HV0,
    KAP, JMP, MOV, REACH, JS0, JD0, W0, G0, K0, JS1, JD1, W1, SP1, st, pt,
    load_sem, ss, rs,
):
    X, Y, Z = p_hbm.shape
    gx, gy = lax.axis_index("gx"), lax.axis_index("gy")
    has = {
        ("x", 0): gx > 0, ("x", 1): gx < nx_dev - 1,
        ("y", 0): gy > 0, ("y", 1): gy < ny_dev - 1,
    }
    device = {
        ("x", 0): {"gx": gx - 1}, ("x", 1): {"gx": gx + 1},
        ("y", 0): {"gy": gy - 1}, ("y", 1): {"gy": gy + 1},
    }

    barrier = pltpu.get_barrier_semaphore()
    count = jnp.int32(0)
    for key, there in has.items():
        @pl.when(there)
        def _():
            pl.semaphore_signal(barrier, inc=1, device_id=device[key], device_id_type=MESH)
        count = count + there.astype(jnp.int32)

    own = pl.ds(1, X)
    loads = []
    for k, (src, dst) in enumerate((
        (p_hbm, P0.at[own]), (m_hbm, M0.at[own]),
        (an_hbm, AN.at[own]), (or_hbm, OR.at[own]), (bm_hbm, BM.at[own]), (st_hbm, st), (pt_hbm, pt),
        (a_hbm, A.at[own]), (b_hbm, B.at[own]),
    )):
        copy = pltpu.make_async_copy(src, dst, load_sem.at[k])
        copy.start()
        loads.append(copy)

    sems = iter(range(ss.shape[0]))

    def exchange(axis, pieces, send_if=None, arrive_if=None):
        there = {side: has[axis, side] for side in (0, 1)}
        send_if, arrive_if = send_if or there, arrive_if or there
        sends = {0: [], 1: []}
        arrivals = {0: [], 1: []}
        for down, down_to, up, up_to in pieces:
            for side, src, dst in ((0, down, down_to), (1, up, up_to)):
                k = next(sems)
                copy = pltpu.make_async_remote_copy(
                    src_ref=src, dst_ref=dst, send_sem=ss.at[k], recv_sem=rs.at[k],
                    device_id=device[axis, side], device_id_type=MESH,
                )
                sends[side].append(copy)
                arrivals[1 - side].append(copy)

        def each(groups, conditions, act):
            def run():
                for side in (0, 1):
                    if groups[side]:
                        @pl.when(conditions[side])
                        def _():
                            for copy in groups[side]:
                                act(copy)
            return run

        return (
            each(sends, send_if, lambda copy: copy.start()),
            each(arrivals, arrive_if, lambda copy: copy.wait_recv()),
            each(sends, send_if, lambda copy: copy.wait_send()),
        )

    def x_faces(ref):
        return ref.at[1], ref.at[X + 1], ref.at[X], ref.at[0]

    inside = pl.ds(2, X - 2)

    def y_faces(ref, aside, layers=own):
        return ref.at[layers, 0], aside.at[layers, 7], ref.at[layers, Y - 1], aside.at[layers, 0]

    x_state = exchange("x", [x_faces(P0), x_faces(M0)])
    y_state = exchange("y", [y_faces(P0, HP0), y_faces(M0, HM0)])
    x_middle = exchange("x", [x_faces(ref) for ref in (P1, M1, U1, V1)])
    y_edge = exchange("y", [(CO.at[0], CI.at[1], CO.at[1], CI.at[0])])
    y_middle = exchange("y", [y_faces(P1, HP1, inside), y_faces(M1, HM1, inside), y_faces(U1, HU1, inside), y_faces(V1, HV1, inside)])
    x_last = exchange("x", [x_faces(ref) for ref in (U0, V0)])
    y_last = exchange("y", [y_faces(U0, HU0), y_faces(V0, HV0)])

    for side, layer in enumerate((0, X + 1)):
        @pl.when(jnp.logical_not(has["x", side]))
        def _():
            for ref in (P0, M0, P1, M1, U1, V1, U0, V0):
                ref[layer] = jnp.zeros((Y, Z), ref.dtype)

    with jax.named_scope("wait_barrier"):
        pl.semaphore_wait(barrier, count)
    pass
    with jax.named_scope("wait_load"):
        loads[0].wait()
        loads[1].wait()
    x_state[0]()
    y_state[0]()
    with jax.named_scope("wait_load_rest"):
        for copy in loads[2:]:
            copy.wait()

    lane = lax.broadcasted_iota(jnp.int32, (8, 128), 1)
    line = lax.broadcasted_iota(jnp.int32, (8, 128), 0)
    first_lane, last_lane, first_line, last_line = lane == 0, lane == 127, line == 0, line == 7

    def shifted(parts, by, size, axis, edge):
        turned = [pltpu.roll(part, by % size, axis) for part in parts]
        return [jnp.where(edge, before, here) for before, here in zip([0.0] + turned, turned)]

    def lap(ref, i, below=True, above=True):
        tiles = [[ref[i, a:a + 8, b:b + 128] for b in range(0, Z, 128)] for a in range(0, Y, 8)]
        result = []
        along_y = []
        for column in zip(*tiles):
            down = shifted(column, 1, 8, 0, first_line)
            up = shifted(column[::-1], -1, 8, 0, last_line)[::-1]
            along_y.append([d + u for d, u in zip(down, up)])
        for a, row in enumerate(tiles):
            left = shifted(row, 1, 128, 1, first_lane)
            right = shifted(row[::-1], -1, 128, 1, last_lane)[::-1]
            result.append(jnp.concatenate(
                [l + r + along_y[b][a] - 6.0 * c for b, (l, r, c) in enumerate(zip(left, right, row))], axis=1
            ))
        beside = jnp.concatenate(result, axis=0)
        if below:
            beside = beside + ref[i - 1]
        if above:
            beside = beside + ref[i + 1]
        return beside

    def tables(i):
        KAP[i] = pick(AN[i], st, st.shape[0])
        JMP[i] = 1.0 - pick(OR[i], pt, pt.shape[0])
        movable = 1.0 - BM[i].astype(jnp.float32)
        MOV[i] = movable
        REACH[i] = mobility_step * movable

    def sensitivities(at, phase):
        jump = JMP[at]
        _, slope, _, release = local_terms(phase, jump)
        spread = B[at] * (MOV[at] * release)
        U1[at] = KAP[at] * (REACH[at] * (A[at] - spread * (jump * slope)))
        V1[at] = diffusion_step * spread

    def forward(i):
        phase, potential = P0[i], M0[i]
        jump = JMP[i]
        t, slope, slope_derivative, release = local_terms(phase, jump)
        held_slope, held_derivative = jump * slope, jump * slope_derivative
        drive = (
            KAP[i] * lap(P0, i)
            - 2.0 * well_height * t * (1.0 - 2.0 * phase)
            + coupling * held_slope * potential
        )
        step = REACH[i] * drive
        yielding = MOV[i] * release
        flux = yielding * (diffusion_step * lap(M0, i) - held_slope * step)
        P1[i] = phase + step
        M1[i] = potential + flux
        JS0[i] = held_slope
        JD0[i] = held_derivative
        W0[i] = yielding
        G0[i] = well_height * (12.0 * t - 2.0) + coupling * held_derivative * potential
        K0[i] = held_slope * flux - held_derivative * step
        sensitivities(i, phase + step)

    def forward_row(i, row, aside):
        here, away = (i, slice(row, row + 1)), (i, slice(aside, aside + 1))
        step = REACH[here] * KAP[here] * HP0[away]
        flux = W0[here] * (diffusion_step * HM0[away] - JS0[here] * step)
        phase = P1[here] + step
        P1[here] = phase
        M1[here] = M1[here] + flux
        K0[here] = K0[here] + JS0[here] * flux - JD0[here] * step
        sensitivities(here, phase)

    def backward(i):
        x = i - 1
        phase, potential = P1[i], M1[i]
        jump, reach = JMP[i], REACH[i]
        t, slope, slope_derivative, release = local_terms(phase, jump)
        held_slope, held_derivative = jump * slope, jump * slope_derivative
        drive = (
            KAP[i] * lap(P1, i)
            - 2.0 * well_height * t * (1.0 - 2.0 * phase)
            + coupling * held_slope * potential
        )
        step = reach * drive
        yielding = MOV[i] * release
        flux = yielding * (diffusion_step * lap(M1, i) - held_slope * step)
        gain = well_height * (12.0 * t - 2.0) + coupling * held_derivative * potential
        keep = held_slope * flux - held_derivative * step
        spread = B[i] * yielding
        pull = reach * (A[i] - spread * held_slope)
        JS1[i] = held_slope
        JD1[i] = held_derivative
        W1[i] = yielding
        SP1[i] = spread
        bar_p = A[i] + pull * gain + spread * keep + lap(U1, i)
        bar_m = B[i] + coupling * held_slope * pull + lap(V1, i)
        spread = bar_m * W0[i]
        pull = reach * (bar_p - spread * JS0[i])
        U0[i] = KAP[i] * pull
        V0[i] = diffusion_step * spread
        out_p[x] = bar_p + pull * G0[i] + spread * K0[i]
        out_m[x] = bar_m + coupling * JS0[i] * pull

    def backward_row(i, row, aside):
        at, here, away = (i - 1, slice(row, row + 1)), (i, slice(row, row + 1)), (i, slice(aside, aside + 1))
        step = REACH[here] * KAP[here] * HP1[away]
        flux = W1[here] * (diffusion_step * HM1[away] - JS1[here] * step)
        bar_p = SP1[here] * (JS1[here] * flux - JD1[here] * step) + HU1[away]
        bar_m = HV1[away]
        spread = bar_m * W0[here]
        pull = REACH[here] * (bar_p - spread * JS0[here])
        U0[here] = U0[here] + KAP[here] * pull
        V0[here] = V0[here] + diffusion_step * spread
        out_p[at] = out_p[at] + (bar_p + pull * G0[here] + spread * K0[here])
        out_m[at] = out_m[at] + (bar_m + coupling * JS0[here] * pull)

    def finish(i, **sides):
        out_p[i - 1] = out_p[i - 1] + lap(U0, i, **sides)
        out_m[i - 1] = out_m[i - 1] + lap(V0, i, **sides)

    def finish_row(i, row, aside):
        at, away = (i - 1, slice(row, row + 1)), (i, slice(aside, aside + 1))
        out_p[at] = out_p[at] + HU0[away]
        out_m[at] = out_m[at] + HV0[away]

    def over(low, high, body, unroll=2):
        def step(x, carry):
            body(x)
            return carry
        lax.fori_loop(low, high, step, 0, unroll=unroll)

    def edges(body):
        over(0, 2, lambda k: body(1 + k * (X - 1)))

    def by_rows(run, body):
        for side, row, aside in ((0, 0, 0), (1, Y - 1, 7)):
            @pl.when(has["y", side])
            def _():
                run(lambda x: body(x, row, aside))

    def inside_rows(body):
        by_rows(lambda act: over(2, X, act, 2), body)

    def edge_rows(body):
        by_rows(edges, body)

    def corners(*refs):
        return [(ref, layer) for ref in refs for layer in (1, X)]

    with jax.named_scope("tables"):
        over(1, X + 1, tables)
    with jax.named_scope("forward_inside"):
        over(2, X, forward)
    def forward_rows():
        inside_rows(forward_row)
        y_middle[0]()

    y_state[1]()
    with jax.named_scope("forward_edges"):
        x_state[1]()
        edges(forward)
        edge_rows(forward_row)
        x_middle[0]()
        for side, row in ((0, 0), (1, Y - 1)):
            for k, (ref, layer) in enumerate(corners(P1, M1, U1, V1)):
                CO[side, k:k + 1] = ref[layer, row:row + 1]
        y_edge[0]()
    with jax.named_scope("forward_rows_late"):
        forward_rows()
    with jax.named_scope("backward_inside"):
        over(2, X, backward)
    with jax.named_scope("backward_edges"):
        y_edge[1]()
        for side, aside in ((0, 0), (1, 7)):
            @pl.when(has["y", side])
            def _():
                for k, (ref, layer) in enumerate(corners(HP1, HM1, HU1, HV1)):
                    ref[layer, aside:aside + 1] = CI[side, k:k + 1]
        x_middle[1]()
        edges(backward)
        edge_rows(backward_row)
        x_last[0]()
    with jax.named_scope("backward_rows"):
        y_middle[1]()
        inside_rows(backward_row)
        y_last[0]()
    with jax.named_scope("finish_inside"):
        over(2, X, finish)
        finish(1, below=False)
        finish(X, above=False)
    with jax.named_scope("finish_rows"):
        y_last[1]()
        by_rows(lambda act: over(1, X + 1, act, 4), finish_row)
    with jax.named_scope("finish_edges"):
        x_last[1]()
        for x, layer in ((0, 0), (X - 1, X + 1)):
            out_p[x] = out_p[x] + U0[layer]
            out_m[x] = out_m[x] + V0[layer]
    with jax.named_scope("wait_sends"):
        for step in (x_state, y_state, x_middle, y_edge, y_middle, x_last, y_last):
            step[2]()


def hand_over(p_ref, m_ref, p_out, m_out, sem):
    copies = [pltpu.make_async_copy(p_ref, p_out, sem.at[0]), pltpu.make_async_copy(m_ref, m_out, sem.at[1])]
    for copy in copies:
        copy.start()
    for copy in copies:
        copy.wait()


def solution(mesh):
    nx_dev, ny_dev = mesh.shape["gx"], mesh.shape["gy"]
    split = P("gx", "gy", None)

    def on_device(*args):
        X, Y, Z = args[0].shape
        f32, i32 = jnp.float32, jnp.int32
        hbm = pl.BlockSpec(memory_space=pltpu.HBM)
        vmem = pltpu.VMEM
        copies = 2 * (2 + 4 + 2) + 2 * (2 + 1 + 4 + 2)
        results = pl.pallas_call(
            functools.partial(kernel, nx_dev, ny_dev),
            out_shape=[vmem((X, Y, Z), f32)] * 2,
            in_specs=[hbm] * 9,
            out_specs=[pl.BlockSpec(memory_space=vmem)] * 2,
            scratch_shapes=(
                [vmem((X + 2, Y, Z), f32)] * 2
                + [vmem((X + 2, Y, Z), i32)] * 3
                + [vmem((X + 2, Y, Z), f32)] * 8
                + [vmem((2, 8, Z), f32)] * 2
                + [vmem((X + 2, 8, Z), f32)] * 8
                + [vmem((X + 2, Y, Z), f32)] * 13
                + [pltpu.SMEM(args[7].shape, f32), pltpu.SMEM(args[8].shape, f32)]
                + [pltpu.SemaphoreType.DMA((9,))]
                + [pltpu.SemaphoreType.DMA((copies,))] * 2
            ),
            compiler_params=pltpu.CompilerParams(
                collective_id=0, has_side_effects=True, vmem_limit_bytes=32 * 1024 * 1024
            ),
            name="reverse",
        )(*[pltpu.with_memory_space_constraint(arg, pltpu.HBM) for arg in args])
        results = [pltpu.with_memory_space_constraint(r, vmem) for r in results]
        return pl.pallas_call(
            hand_over,
            out_shape=[jax.ShapeDtypeStruct((X, Y, Z), f32)] * 2,
            in_specs=[pl.BlockSpec(memory_space=vmem)] * 2,
            out_specs=[hbm] * 2,
            scratch_shapes=[pltpu.SemaphoreType.DMA((2,))],
            name="hand_over",
        )(*results)

    return jax.shard_map(
        on_device, mesh=mesh, in_specs=(split,) * 7 + (P(), P()), out_specs=(split, split), check_vma=False
    )
```

```python
import functools

import jax
import jax.numpy as jnp
from jax import lax
from jax.experimental import pallas as pl
from jax.experimental.pallas import tpu as pltpu
from jax.sharding import PartitionSpec as P

mobility_step = 0.1
well_height = 1.0
coupling = 1.0
diffusion_step = 0.03

MESH = pl.DeviceIdType.MESH
RUN = 4


def pick(index, table, count):
    values = [table[k] for k in range(count)]
    bit = 1
    while len(values) > 1:
        odd = (index & bit) != 0
        values = [jnp.where(odd, values[k + 1], values[k]) for k in range(0, len(values), 2)]
        bit *= 2
    return values[0]


def local_terms(phase, jump):
    t = phase - phase * phase
    denominator = 1.0 - 2.0 * t
    rest = denominator - jump * (phase - t)
    both = 1.0 / (denominator * rest)
    inverse = rest * both
    release = denominator * (denominator * both)
    square = inverse * inverse
    slope = 2.0 * t * square
    slope_derivative = (2.0 - 4.0 * phase) * (1.0 + 2.0 * t) * (square * inverse)
    return t, slope, slope_derivative, release


def kernel(
    nx_dev, ny_dev,
    p_hbm, m_hbm, a_hbm, b_hbm, or_hbm, an_hbm, bm_hbm, st_hbm, pt_hbm,
    out_p, out_m,
    A, B, OR, AN, BM, P0, M0, P1, M1, U1, V1, U0, V0, CO, CI, DO, DI, HP0, HM0, HP1, HM1, HU1, HV1, HU0, HV0,
    KAP, JMP, MOV, REACH, JS0, JD0, W0, G0, K0, JS1, JD1, W1, SP1, st, pt,
    load_sem, ss, rs, ready,
):
    X, Y, Z = p_hbm.shape
    gx, gy = lax.axis_index("gx"), lax.axis_index("gy")
    has = {
        ("x", 0): gx > 0, ("x", 1): gx < nx_dev - 1,
        ("y", 0): gy > 0, ("y", 1): gy < ny_dev - 1,
    }
    device = {
        ("x", 0): {"gx": gx - 1}, ("x", 1): {"gx": gx + 1},
        ("y", 0): {"gy": gy - 1}, ("y", 1): {"gy": gy + 1},
    }

    at, even = lax.rem(gx, RUN), lax.rem(gy, 2) == 0
    odd, begins, ends = jnp.logical_not(even), at == 0, at == RUN - 1
    mutual = {("x", 0): has["x", 0] & begins & odd, ("x", 1): has["x", 1] & ends & odd}
    caller = begins ^ even
    calls = {
        ("x", 0): has["x", 0] & (begins | ends), ("x", 1): (has["x", 1] & (at < 2)) | mutual["x", 1],
        ("y", 0): has["y", 0] & caller, ("y", 1): has["y", 1] & caller,
    }
    called = {key: has[key] & jnp.logical_not(calls[key]) for key in has}
    asks = dict(calls)
    asks["x", 0] = calls["x", 0] & jnp.logical_not(mutual["x", 0])
    asks["x", 1] = calls["x", 1] & jnp.logical_not(mutual["x", 1])
    answer = {key: k for k, key in enumerate(has)}

    barrier = pltpu.get_barrier_semaphore()
    count = jnp.int32(0)
    for key in has:
        @pl.when(calls[key])
        def _():
            pl.semaphore_signal(barrier, inc=1, device_id=device[key], device_id_type=MESH)
        count = count + called[key].astype(jnp.int32)
    count = count + mutual["x", 1].astype(jnp.int32)

    own = pl.ds(1, X)
    loads = []
    for k, (src, dst) in enumerate((
        (p_hbm, P0.at[own]), (m_hbm, M0.at[own]),
        (an_hbm, AN.at[own]), (or_hbm, OR.at[own]), (bm_hbm, BM.at[own]), (st_hbm, st), (pt_hbm, pt),
        (a_hbm, A.at[own]), (b_hbm, B.at[own]),
    )):
        copy = pltpu.make_async_copy(src, dst, load_sem.at[k])
        copy.start()
        loads.append(copy)

    sems = iter(range(ss.shape[0]))

    def exchange(axis, pieces, send_if=None, arrive_if=None):
        there = {side: has[axis, side] for side in (0, 1)}
        send_if, arrive_if = send_if or there, arrive_if or there
        sends = {0: [], 1: []}
        arrivals = {0: [], 1: []}
        for down, down_to, up, up_to in pieces:
            for side, src, dst in ((0, down, down_to), (1, up, up_to)):
                k = next(sems)
                copy = pltpu.make_async_remote_copy(
                    src_ref=src, dst_ref=dst, send_sem=ss.at[k], recv_sem=rs.at[k],
                    device_id=device[axis, side], device_id_type=MESH,
                )
                sends[side].append(copy)
                arrivals[1 - side].append(copy)

        def each(groups, conditions, act):
            def run(sides=(0, 1)):
                for side in sides:
                    @pl.when(conditions[side])
                    def _():
                        for copy in groups[side]:
                            act(copy)
            return run

        return (
            each(sends, send_if, lambda copy: copy.start()),
            each(arrivals, arrive_if, lambda copy: copy.wait_recv()),
            each(sends, send_if, lambda copy: copy.wait_send()),
        )

    def x_faces(ref):
        return ref.at[1], ref.at[X + 1], ref.at[X], ref.at[0]

    inside = pl.ds(2, X - 2)

    def y_faces(ref, aside, layers=own):
        return ref.at[layers, 0], aside.at[layers, 7], ref.at[layers, Y - 1], aside.at[layers, 0]

    x_state = exchange("x", [
        (ref.at[1], ref.at[X + 1], src.at[X - 1], ref.at[0]) for src, ref in ((p_hbm, P0), (m_hbm, M0))
    ])
    y_state = exchange("y", [y_faces(P0, HP0), y_faces(M0, HM0)])
    x_middle = exchange("x", [x_faces(ref) for ref in (P1, M1, U1, V1)])
    y_edge = exchange("y", [(CO.at[0], CI.at[1], CO.at[1], CI.at[0])])
    y_middle = exchange("y", [y_faces(P1, HP1, inside), y_faces(M1, HM1, inside), y_faces(U1, HU1, inside), y_faces(V1, HV1, inside)])
    x_last = exchange("x", [x_faces(ref) for ref in (U0, V0)])
    y_last = exchange("y", [y_faces(U0, HU0, inside), y_faces(V0, HV0, inside)])
    y_last_edge = exchange("y", [(DO.at[0], DI.at[1], DO.at[1], DI.at[0])])

    for side, layer in enumerate((0, X + 1)):
        @pl.when(jnp.logical_not(has["x", side]))
        def _():
            for ref in (P0, M0, P1, M1, U1, V1, U0, V0):
                ref[layer] = jnp.zeros((Y, Z), ref.dtype)

    pl.when(count > 0)(lambda: pl.semaphore_wait(barrier, count))
    for axis, side in has:
        @pl.when(called[axis, side])
        def _():
            pl.semaphore_signal(
                ready.at[answer[axis, 1 - side]], inc=1, device_id=device[axis, side], device_id_type=MESH
            )

    def wait_answer(key):
        pl.semaphore_wait(ready.at[answer[key]], 1)

    pl.when(called["x", 1] | mutual["x", 1])(lambda: x_state[0]((1,)))
    loads[0].wait()
    loads[1].wait()
    pl.when(called["x", 0])(lambda: x_state[0]((0,)))
    for side in (0, 1):
        pl.when(asks["y", side])(lambda: wait_answer(("y", side)))
        y_state[0]((side,))

    @pl.when(asks["x", 0] & ends)
    def _():
        wait_answer(("x", 0))
        x_state[0]((0,))

    for copy in loads[2:]:
        copy.wait()

    lane = lax.broadcasted_iota(jnp.int32, (8, 128), 1)
    line = lax.broadcasted_iota(jnp.int32, (8, 128), 0)
    first_lane, last_lane, first_line, last_line = lane == 0, lane == 127, line == 0, line == 7

    def shifted(parts, by, size, axis, edge):
        turned = [pltpu.roll(part, by % size, axis) for part in parts]
        return [jnp.where(edge, before, here) for before, here in zip([0.0] + turned, turned)]

    def lap(ref, i, below=True, above=True):
        tiles = [[ref[i, a:a + 8, b:b + 128] for b in range(0, Z, 128)] for a in range(0, Y, 8)]
        result = []
        along_y = []
        for column in zip(*tiles):
            down = shifted(column, 1, 8, 0, first_line)
            up = shifted(column[::-1], -1, 8, 0, last_line)[::-1]
            along_y.append([d + u for d, u in zip(down, up)])
        for a, row in enumerate(tiles):
            left = shifted(row, 1, 128, 1, first_lane)
            right = shifted(row[::-1], -1, 128, 1, last_lane)[::-1]
            result.append(jnp.concatenate(
                [l + r + along_y[b][a] - 6.0 * c for b, (l, r, c) in enumerate(zip(left, right, row))], axis=1
            ))
        beside = jnp.concatenate(result, axis=0)
        if below:
            beside = beside + ref[i - 1]
        if above:
            beside = beside + ref[i + 1]
        return beside

    def tables(i):
        KAP[i] = pick(AN[i], st, st.shape[0])
        JMP[i] = 1.0 - pick(OR[i], pt, pt.shape[0])
        movable = 1.0 - BM[i].astype(jnp.float32)
        MOV[i] = movable
        REACH[i] = mobility_step * movable

    def sensitivities(at, phase):
        jump = JMP[at]
        _, slope, _, release = local_terms(phase, jump)
        spread = B[at] * (MOV[at] * release)
        U1[at] = KAP[at] * (REACH[at] * (A[at] - spread * (jump * slope)))
        V1[at] = diffusion_step * spread

    def forward(i):
        phase, potential = P0[i], M0[i]
        jump = JMP[i]
        t, slope, slope_derivative, release = local_terms(phase, jump)
        held_slope, held_derivative = jump * slope, jump * slope_derivative
        drive = (
            KAP[i] * lap(P0, i)
            - 2.0 * well_height * t * (1.0 - 2.0 * phase)
            + coupling * held_slope * potential
        )
        step = REACH[i] * drive
        yielding = MOV[i] * release
        flux = yielding * (diffusion_step * lap(M0, i) - held_slope * step)
        P1[i] = phase + step
        M1[i] = potential + flux
        JS0[i] = held_slope
        JD0[i] = held_derivative
        W0[i] = yielding
        G0[i] = well_height * (12.0 * t - 2.0) + coupling * held_derivative * potential
        K0[i] = held_slope * flux - held_derivative * step
        sensitivities(i, phase + step)

    def forward_row(i, row, aside):
        here, away = (i, slice(row, row + 1)), (i, slice(aside, aside + 1))
        step = REACH[here] * KAP[here] * HP0[away]
        flux = W0[here] * (diffusion_step * HM0[away] - JS0[here] * step)
        phase = P1[here] + step
        P1[here] = phase
        M1[here] = M1[here] + flux
        K0[here] = K0[here] + JS0[here] * flux - JD0[here] * step
        sensitivities(here, phase)

    def backward(i):
        x = i - 1
        phase, potential = P1[i], M1[i]
        jump, reach = JMP[i], REACH[i]
        t, slope, slope_derivative, release = local_terms(phase, jump)
        held_slope, held_derivative = jump * slope, jump * slope_derivative
        drive = (
            KAP[i] * lap(P1, i)
            - 2.0 * well_height * t * (1.0 - 2.0 * phase)
            + coupling * held_slope * potential
        )
        step = reach * drive
        yielding = MOV[i] * release
        flux = yielding * (diffusion_step * lap(M1, i) - held_slope * step)
        gain = well_height * (12.0 * t - 2.0) + coupling * held_derivative * potential
        keep = held_slope * flux - held_derivative * step
        spread = B[i] * yielding
        pull = reach * (A[i] - spread * held_slope)
        JS1[i] = held_slope
        JD1[i] = held_derivative
        W1[i] = yielding
        SP1[i] = spread
        bar_p = A[i] + pull * gain + spread * keep + lap(U1, i)
        bar_m = B[i] + coupling * held_slope * pull + lap(V1, i)
        spread = bar_m * W0[i]
        pull = reach * (bar_p - spread * JS0[i])
        U0[i] = KAP[i] * pull
        V0[i] = diffusion_step * spread
        out_p[x] = bar_p + pull * G0[i] + spread * K0[i]
        out_m[x] = bar_m + coupling * JS0[i] * pull

    def backward_row(i, row, aside):
        at, here, away = (i - 1, slice(row, row + 1)), (i, slice(row, row + 1)), (i, slice(aside, aside + 1))
        step = REACH[here] * KAP[here] * HP1[away]
        flux = W1[here] * (diffusion_step * HM1[away] - JS1[here] * step)
        bar_p = SP1[here] * (JS1[here] * flux - JD1[here] * step) + HU1[away]
        bar_m = HV1[away]
        spread = bar_m * W0[here]
        pull = REACH[here] * (bar_p - spread * JS0[here])
        U0[here] = U0[here] + KAP[here] * pull
        V0[here] = V0[here] + diffusion_step * spread
        out_p[at] = out_p[at] + (bar_p + pull * G0[here] + spread * K0[here])
        out_m[at] = out_m[at] + (bar_m + coupling * JS0[here] * pull)

    def finish(i, **sides):
        out_p[i - 1] = out_p[i - 1] + lap(U0, i, **sides)
        out_m[i - 1] = out_m[i - 1] + lap(V0, i, **sides)

    def finish_row(i, row, aside):
        at, away = (i - 1, slice(row, row + 1)), (i, slice(aside, aside + 1))
        out_p[at] = out_p[at] + HU0[away]
        out_m[at] = out_m[at] + HV0[away]

    def over(low, high, body, unroll=2):
        def step(x, carry):
            body(x)
            return carry
        lax.fori_loop(low, high, step, 0, unroll=unroll)

    def edges(body):
        over(0, 2, lambda k: body(1 + k * (X - 1)))

    def by_rows(run, body):
        for side, row, aside in ((0, 0, 0), (1, Y - 1, 7)):
            @pl.when(has["y", side])
            def _():
                run(lambda x: body(x, row, aside))

    def inside_rows(body):
        by_rows(lambda act: over(2, X, act, 2), body)

    def edge_rows(body):
        by_rows(edges, body)

    def corners(*refs):
        return [(ref, layer) for ref in refs for layer in (1, X)]

    with jax.named_scope("tables"):
        over(1, X + 1, tables)
    with jax.named_scope("forward_inside"):
        over(2, X, forward)
        @pl.when(asks["x", 1])
        def _():
            wait_answer(("x", 1))
            x_state[0]((1,))

        @pl.when(asks["x", 0] & begins)
        def _():
            wait_answer(("x", 0))
            x_state[0]((0,))

        @pl.when(mutual["x", 0])
        def _():
            pl.semaphore_wait(barrier, 1)
            x_state[0]((0,))

    def by_sides(body, upper_first):
        pl.when(upper_first)(lambda: body(1, X))
        body(0, 1)
        pl.when(jnp.logical_not(upper_first))(lambda: body(1, X))

    def pack(buffer, *refs):
        for side, row in ((0, 0), (1, Y - 1)):
            for k, (ref, layer) in enumerate(corners(*refs)):
                buffer[side, k:k + 1] = ref[layer, row:row + 1]

    def unpack(buffer, *refs):
        for side, aside in ((0, 0), (1, 7)):
            @pl.when(has["y", side])
            def _():
                for k, (ref, layer) in enumerate(corners(*refs)):
                    ref[layer, aside:aside + 1] = buffer[side, k:k + 1]

    def forward_edge(side, layer):
        x_state[1]((side,))
        forward(layer)
        by_rows(lambda act: act(layer), forward_row)
        x_middle[0]((side,))

    def backward_edge(side, layer):
        x_middle[1]((side,))
        backward(layer)
        by_rows(lambda act: act(layer), backward_row)
        x_last[0]((side,))

    with jax.named_scope("forward_edges"):
        y_state[1]()
        by_sides(forward_edge, begins)
        pack(CO, P1, M1, U1, V1)
        y_edge[0]()
    with jax.named_scope("forward_rows"):
        inside_rows(forward_row)
        y_middle[0]()
    with jax.named_scope("backward_inside"):
        over(2, X, backward)
    with jax.named_scope("backward_edges"):
        y_edge[1]()
        unpack(CI, HP1, HM1, HU1, HV1)
        by_sides(backward_edge, begins | ends)
        pack(DO, U0, V0)
        y_last_edge[0]()
    with jax.named_scope("backward_rows"):
        y_middle[1]()
        inside_rows(backward_row)
        y_last[0]()
    with jax.named_scope("finish_inside"):
        over(2, X, finish)
        finish(1, below=False)
        finish(X, above=False)
        for step in (x_state, y_state, x_middle, y_edge, y_middle):
            step[2]()
    with jax.named_scope("finish_rows"):
        y_last[1]()
        inside_rows(finish_row)
        y_last_edge[1]()
        unpack(DI, HU0, HV0)
        edge_rows(finish_row)
    with jax.named_scope("finish_edges"):
        x_last[1]()
        for x, layer in ((0, 0), (X - 1, X + 1)):
            out_p[x] = out_p[x] + U0[layer]
            out_m[x] = out_m[x] + V0[layer]
    with jax.named_scope("wait_sends"):
        for step in (x_last, y_last, y_last_edge):
            step[2]()


def hand_over(p_ref, m_ref, p_out, m_out, sem):
    copies = [pltpu.make_async_copy(p_ref, p_out, sem.at[0]), pltpu.make_async_copy(m_ref, m_out, sem.at[1])]
    for copy in copies:
        copy.start()
    for copy in copies:
        copy.wait()


def solution(mesh):
    nx_dev, ny_dev = mesh.shape["gx"], mesh.shape["gy"]
    split = P("gx", "gy", None)

    def on_device(*args):
        X, Y, Z = args[0].shape
        f32, i32 = jnp.float32, jnp.int32
        hbm = pl.BlockSpec(memory_space=pltpu.HBM)
        vmem = pltpu.VMEM
        copies = 2 * (2 + 4 + 2) + 2 * (2 + 1 + 4 + 2 + 1)
        results = pl.pallas_call(
            functools.partial(kernel, nx_dev, ny_dev),
            out_shape=[vmem((X, Y, Z), f32)] * 2,
            in_specs=[hbm] * 9,
            out_specs=[pl.BlockSpec(memory_space=vmem)] * 2,
            scratch_shapes=(
                [vmem((X + 2, Y, Z), f32)] * 2
                + [vmem((X + 2, Y, Z), i32)] * 3
                + [vmem((X + 2, Y, Z), f32)] * 8
                + [vmem((2, 8, Z), f32)] * 4
                + [vmem((X + 2, 8, Z), f32)] * 8
                + [vmem((X + 2, Y, Z), f32)] * 13
                + [pltpu.SMEM(args[7].shape, f32), pltpu.SMEM(args[8].shape, f32)]
                + [pltpu.SemaphoreType.DMA((9,))]
                + [pltpu.SemaphoreType.DMA((copies,))] * 2
                + [pltpu.SemaphoreType.REGULAR((4,))]
            ),
            compiler_params=pltpu.CompilerParams(
                collective_id=0, has_side_effects=True, vmem_limit_bytes=32 * 1024 * 1024
            ),
            name="reverse",
        )(*[pltpu.with_memory_space_constraint(arg, pltpu.HBM) for arg in args])
        results = [pltpu.with_memory_space_constraint(r, vmem) for r in results]
        return pl.pallas_call(
            hand_over,
            out_shape=[jax.ShapeDtypeStruct((X, Y, Z), f32)] * 2,
            in_specs=[pl.BlockSpec(memory_space=vmem)] * 2,
            out_specs=[hbm] * 2,
            scratch_shapes=[pltpu.SemaphoreType.DMA((2,))],
            name="hand_over",
        )(*results)

    return jax.shard_map(
        on_device, mesh=mesh, in_specs=(split,) * 7 + (P(), P()), out_specs=(split, split), check_vma=False
    )
```

```python
import functools

import jax
import jax.numpy as jnp
from jax import lax
from jax.experimental import pallas as pl
from jax.experimental.pallas import tpu as pltpu
from jax.sharding import PartitionSpec as P

mobility_step = 0.1
well_height = 1.0
coupling = 1.0
diffusion_step = 0.03

MESH = pl.DeviceIdType.MESH
RUN = 4


def pick(index, table, count):
    values = [table[k] for k in range(count)]
    bit = 1
    while len(values) > 1:
        odd = (index & bit) != 0
        values = [jnp.where(odd, values[k + 1], values[k]) for k in range(0, len(values), 2)]
        bit *= 2
    return values[0]


def local_terms(phase, jump):
    t = phase - phase * phase
    denominator = 1.0 - 2.0 * t
    rest = denominator - jump * (phase - t)
    both = 1.0 / (denominator * rest)
    inverse = rest * both
    release = denominator * (denominator * both)
    square = inverse * inverse
    slope = 2.0 * t * square
    slope_derivative = (2.0 - 4.0 * phase) * (1.0 + 2.0 * t) * (square * inverse)
    return t, slope, slope_derivative, release


def kernel(
    nx_dev, ny_dev,
    p_hbm, m_hbm, a_hbm, b_hbm, or_hbm, an_hbm, bm_hbm, st_hbm, pt_hbm,
    out_p, out_m,
    A, B, OR, AN, BM, S0, S1, S2, H0, H1, H2,
    KAP, JMP, MOV, REACH, JS0, JD0, W0, G0, K0, JS1, JD1, W1, SP1, st, pt,
    load_sem, ss, rs, ready,
):
    X, Y, Z = p_hbm.shape
    P0, M0, HP0, HM0 = S0.at[:, 0], S0.at[:, 1], H0.at[:, 0], H0.at[:, 1]
    P1, M1, U1, V1 = (S1.at[:, k] for k in range(4))
    HP1, HM1, HU1, HV1 = (H1.at[:, k] for k in range(4))
    U0, V0, HU0, HV0 = S2.at[:, 0], S2.at[:, 1], H2.at[:, 0], H2.at[:, 1]
    gx, gy = lax.axis_index("gx"), lax.axis_index("gy")
    has = {
        ("x", 0): gx > 0, ("x", 1): gx < nx_dev - 1,
        ("y", 0): gy > 0, ("y", 1): gy < ny_dev - 1,
    }
    device = {
        ("x", 0): {"gx": gx - 1}, ("x", 1): {"gx": gx + 1},
        ("y", 0): {"gy": gy - 1}, ("y", 1): {"gy": gy + 1},
    }

    at, even = lax.rem(gx, RUN), lax.rem(gy, 2) == 0
    odd, begins, ends = jnp.logical_not(even), at == 0, at == RUN - 1
    mutual = {("x", 0): has["x", 0] & begins & odd, ("x", 1): has["x", 1] & ends & odd}
    caller = begins ^ even
    calls = {
        ("x", 0): has["x", 0] & (begins | ends), ("x", 1): (has["x", 1] & (at < 2)) | mutual["x", 1],
        ("y", 0): has["y", 0] & caller, ("y", 1): has["y", 1] & caller,
    }
    called = {key: has[key] & jnp.logical_not(calls[key]) for key in has}
    asks = dict(calls)
    asks["x", 0] = calls["x", 0] & jnp.logical_not(mutual["x", 0])
    asks["x", 1] = calls["x", 1] & jnp.logical_not(mutual["x", 1])
    answer = {key: k for k, key in enumerate(has)}

    barrier = pltpu.get_barrier_semaphore()
    count = jnp.int32(0)
    for key in has:
        @pl.when(calls[key])
        def _():
            pl.semaphore_signal(barrier, inc=1, device_id=device[key], device_id_type=MESH)
        count = count + called[key].astype(jnp.int32)
    count = count + mutual["x", 1].astype(jnp.int32)

    own = pl.ds(1, X)
    loads = []
    for k, (src, dst) in enumerate((
        (p_hbm, S0.at[own, 0]), (m_hbm, S0.at[own, 1]),
        (an_hbm, AN.at[own]), (or_hbm, OR.at[own]), (bm_hbm, BM.at[own]), (st_hbm, st), (pt_hbm, pt),
        (a_hbm, A.at[own]), (b_hbm, B.at[own]),
    )):
        copy = pltpu.make_async_copy(src, dst, load_sem.at[k])
        copy.start()
        loads.append(copy)

    sems = iter(range(ss.shape[0]))

    def exchange(axis, pieces, send_if=None, arrive_if=None):
        there = {side: has[axis, side] for side in (0, 1)}
        send_if, arrive_if = send_if or there, arrive_if or there
        sends = {0: [], 1: []}
        arrivals = {0: [], 1: []}
        for down, down_to, up, up_to in pieces:
            for side, src, dst in ((0, down, down_to), (1, up, up_to)):
                if src is None:
                    continue
                k = next(sems)
                copy = pltpu.make_async_remote_copy(
                    src_ref=src, dst_ref=dst, send_sem=ss.at[k], recv_sem=rs.at[k],
                    device_id=device[axis, side], device_id_type=MESH,
                )
                sends[side].append(copy)
                arrivals[1 - side].append(copy)

        def each(groups, conditions, act):
            def run(sides=(0, 1)):
                for side in sides:
                    @pl.when(conditions[side])
                    def _():
                        for copy in groups[side]:
                            act(copy)
            return run

        return (
            each(sends, send_if, lambda copy: copy.start()),
            each(arrivals, arrive_if, lambda copy: copy.wait_recv()),
            each(sends, send_if, lambda copy: copy.wait_send()),
        )

    def x_faces(ref):
        return ref.at[1], ref.at[X + 1], ref.at[X], ref.at[0]

    inside = pl.ds(2, X - 2)

    def y_faces(ref, aside, layers=own):
        return ref.at[layers, :, 0], aside.at[layers, :, 7], ref.at[layers, :, Y - 1], aside.at[layers, :, 0]

    x_state = exchange("x", [
        (S0.at[1], S0.at[X + 1], None, None),
        (None, None, p_hbm.at[X - 1], S0.at[0, 0]),
        (None, None, m_hbm.at[X - 1], S0.at[0, 1]),
    ])
    y_state = exchange("y", [y_faces(S0, H0)])
    x_middle = exchange("x", [x_faces(S1)])
    y_edge = [exchange("y", [y_faces(S1, H1, layer)]) for layer in (1, X)]
    y_middle = exchange("y", [y_faces(S1, H1, inside)])
    x_last = exchange("x", [x_faces(S2)])
    y_last = exchange("y", [y_faces(S2, H2, inside)])
    y_last_edge = [exchange("y", [y_faces(S2, H2, layer)]) for layer in (1, X)]

    for side, layer in enumerate((0, X + 1)):
        @pl.when(jnp.logical_not(has["x", side]))
        def _():
            for ref in (S0, S1, S2):
                ref[layer] = jnp.zeros(ref.shape[1:], ref.dtype)
    for side, row in ((0, 0), (1, 7)):
        @pl.when(jnp.logical_not(has["y", side]))
        def _():
            for ref in (H0, H1):
                for layer in (1, X):
                    ref[layer, :, row:row + 1] = jnp.zeros((ref.shape[1], 1, Z), ref.dtype)

    pl.when(count > 0)(lambda: pl.semaphore_wait(barrier, count))
    for axis, side in has:
        @pl.when(called[axis, side])
        def _():
            pl.semaphore_signal(
                ready.at[answer[axis, 1 - side]], inc=1, device_id=device[axis, side], device_id_type=MESH
            )

    def wait_answer(key):
        pl.semaphore_wait(ready.at[answer[key]], 1)

    pl.when(called["x", 1] | mutual["x", 1])(lambda: x_state[0]((1,)))
    loads[0].wait()
    loads[1].wait()
    pl.when(called["x", 0])(lambda: x_state[0]((0,)))
    for side in (0, 1):
        pl.when(asks["y", side])(lambda: wait_answer(("y", side)))
        y_state[0]((side,))

    @pl.when(asks["x", 0] & ends)
    def _():
        wait_answer(("x", 0))
        x_state[0]((0,))

    for copy in loads[2:]:
        copy.wait()

    lane = lax.broadcasted_iota(jnp.int32, (8, 128), 1)
    line = lax.broadcasted_iota(jnp.int32, (8, 128), 0)
    first_lane, last_lane, first_line, last_line = lane == 0, lane == 127, line == 0, line == 7

    def shifted(parts, by, size, axis, edge):
        turned = [pltpu.roll(part, by % size, axis) for part in parts]
        return [jnp.where(edge, before, here) for before, here in zip([0.0] + turned, turned)]

    def lap(ref, i, below=True, above=True, aside=None):
        tiles = [[ref[i, a:a + 8, b:b + 128] for b in range(0, Z, 128)] for a in range(0, Y, 8)]
        result = []
        along_y = []
        for column in zip(*tiles):
            down = shifted(column, 1, 8, 0, first_line)
            up = shifted(column[::-1], -1, 8, 0, last_line)[::-1]
            along_y.append([d + u for d, u in zip(down, up)])
        if aside is not None:
            for b, column in enumerate(along_y):
                beyond = aside[i, :, 128 * b:128 * (b + 1)]
                column[0] = column[0] + jnp.where(first_line, beyond, 0.0)
                column[-1] = column[-1] + jnp.where(last_line, beyond, 0.0)
        for a, row in enumerate(tiles):
            left = shifted(row, 1, 128, 1, first_lane)
            right = shifted(row[::-1], -1, 128, 1, last_lane)[::-1]
            result.append(jnp.concatenate(
                [l + r + along_y[b][a] - 6.0 * c for b, (l, r, c) in enumerate(zip(left, right, row))], axis=1
            ))
        beside = jnp.concatenate(result, axis=0)
        if below:
            beside = beside + ref[i - 1]
        if above:
            beside = beside + ref[i + 1]
        return beside

    def tables(i):
        KAP[i] = pick(AN[i], st, st.shape[0])
        JMP[i] = 1.0 - pick(OR[i], pt, pt.shape[0])
        movable = 1.0 - BM[i].astype(jnp.float32)
        MOV[i] = movable
        REACH[i] = mobility_step * movable

    def sensitivities(at, phase):
        jump = JMP[at]
        _, slope, _, release = local_terms(phase, jump)
        spread = B[at] * (MOV[at] * release)
        U1[at] = KAP[at] * (REACH[at] * (A[at] - spread * (jump * slope)))
        V1[at] = diffusion_step * spread

    def forward(i, aside=(None, None)):
        phase, potential = P0[i], M0[i]
        jump = JMP[i]
        t, slope, slope_derivative, release = local_terms(phase, jump)
        held_slope, held_derivative = jump * slope, jump * slope_derivative
        drive = (
            KAP[i] * lap(P0, i, aside=aside[0])
            - 2.0 * well_height * t * (1.0 - 2.0 * phase)
            + coupling * held_slope * potential
        )
        step = REACH[i] * drive
        yielding = MOV[i] * release
        flux = yielding * (diffusion_step * lap(M0, i, aside=aside[1]) - held_slope * step)
        P1[i] = phase + step
        M1[i] = potential + flux
        JS0[i] = held_slope
        JD0[i] = held_derivative
        W0[i] = yielding
        G0[i] = well_height * (12.0 * t - 2.0) + coupling * held_derivative * potential
        K0[i] = held_slope * flux - held_derivative * step
        sensitivities(i, phase + step)

    def forward_row(i, row, aside):
        here, away = (i, slice(row, row + 1)), (i, slice(aside, aside + 1))
        step = REACH[here] * KAP[here] * HP0[away]
        flux = W0[here] * (diffusion_step * HM0[away] - JS0[here] * step)
        phase = P1[here] + step
        P1[here] = phase
        M1[here] = M1[here] + flux
        K0[here] = K0[here] + JS0[here] * flux - JD0[here] * step
        sensitivities(here, phase)

    def backward(i, aside=(None, None, None, None)):
        x = i - 1
        phase, potential = P1[i], M1[i]
        jump, reach = JMP[i], REACH[i]
        t, slope, slope_derivative, release = local_terms(phase, jump)
        held_slope, held_derivative = jump * slope, jump * slope_derivative
        drive = (
            KAP[i] * lap(P1, i, aside=aside[0])
            - 2.0 * well_height * t * (1.0 - 2.0 * phase)
            + coupling * held_slope * potential
        )
        step = reach * drive
        yielding = MOV[i] * release
        flux = yielding * (diffusion_step * lap(M1, i, aside=aside[1]) - held_slope * step)
        gain = well_height * (12.0 * t - 2.0) + coupling * held_derivative * potential
        keep = held_slope * flux - held_derivative * step
        spread = B[i] * yielding
        pull = reach * (A[i] - spread * held_slope)
        JS1[i] = held_slope
        JD1[i] = held_derivative
        W1[i] = yielding
        SP1[i] = spread
        bar_p = A[i] + pull * gain + spread * keep + lap(U1, i, aside=aside[2])
        bar_m = B[i] + coupling * held_slope * pull + lap(V1, i, aside=aside[3])
        spread = bar_m * W0[i]
        pull = reach * (bar_p - spread * JS0[i])
        U0[i] = KAP[i] * pull
        V0[i] = diffusion_step * spread
        out_p[x] = bar_p + pull * G0[i] + spread * K0[i]
        out_m[x] = bar_m + coupling * JS0[i] * pull

    def backward_row(i, row, aside):
        at, here, away = (i - 1, slice(row, row + 1)), (i, slice(row, row + 1)), (i, slice(aside, aside + 1))
        step = REACH[here] * KAP[here] * HP1[away]
        flux = W1[here] * (diffusion_step * HM1[away] - JS1[here] * step)
        bar_p = SP1[here] * (JS1[here] * flux - JD1[here] * step) + HU1[away]
        bar_m = HV1[away]
        spread = bar_m * W0[here]
        pull = REACH[here] * (bar_p - spread * JS0[here])
        U0[here] = U0[here] + KAP[here] * pull
        V0[here] = V0[here] + diffusion_step * spread
        out_p[at] = out_p[at] + (bar_p + pull * G0[here] + spread * K0[here])
        out_m[at] = out_m[at] + (bar_m + coupling * JS0[here] * pull)

    def finish(i, **sides):
        out_p[i - 1] = out_p[i - 1] + lap(U0, i, **sides)
        out_m[i - 1] = out_m[i - 1] + lap(V0, i, **sides)

    def finish_row(i, row, aside):
        at, away = (i - 1, slice(row, row + 1)), (i, slice(aside, aside + 1))
        out_p[at] = out_p[at] + HU0[away]
        out_m[at] = out_m[at] + HV0[away]

    def over(low, high, body, unroll=2):
        def step(x, carry):
            body(x)
            return carry
        lax.fori_loop(low, high, step, 0, unroll=unroll)

    def edges(body):
        over(0, 2, lambda k: body(1 + k * (X - 1)))

    def by_rows(run, body):
        for side, row, aside in ((0, 0, 0), (1, Y - 1, 7)):
            @pl.when(has["y", side])
            def _():
                run(lambda x: body(x, row, aside))

    def inside_rows(body):
        by_rows(lambda act: over(2, X, act, 2), body)

    def edge_rows(body):
        by_rows(edges, body)

    with jax.named_scope("tables"):
        over(1, X + 1, tables)
    with jax.named_scope("forward_inside"):
        over(2, X, forward)
        @pl.when(asks["x", 1])
        def _():
            wait_answer(("x", 1))
            x_state[0]((1,))

        @pl.when(asks["x", 0] & begins)
        def _():
            wait_answer(("x", 0))
            x_state[0]((0,))

        @pl.when(mutual["x", 0])
        def _():
            pl.semaphore_wait(barrier, 1)
            x_state[0]((0,))

    def by_sides(body, upper_first, between=None):
        def do_between(order):
            if between is not None:
                pl.when(order & between[1])(between[0])

        lower_first = jnp.logical_not(upper_first)
        pl.when(upper_first)(lambda: body(1, X))
        do_between(upper_first)
        body(0, 1)
        do_between(lower_first)
        pl.when(lower_first)(lambda: body(1, X))

    def forward_edge(side, layer):
        x_state[1]((side,))
        forward(layer, (HP0, HM0))
        x_middle[0]((side,))
        y_edge[side][0]()

    def backward_edge(side, layer):
        y_edge[side][1]()
        x_middle[1]((side,))
        backward(layer, (HP1, HM1, HU1, HV1))
        x_last[0]((side,))
        y_last_edge[side][0]()

    def backward_rows():
        y_middle[1]()
        inside_rows(backward_row)
        y_last[0]()

    rows_between = at < 2

    with jax.named_scope("forward_edges"):
        y_state[1]()
        by_sides(forward_edge, begins)
    with jax.named_scope("forward_rows"):
        inside_rows(forward_row)
        y_middle[0]()
    with jax.named_scope("backward_inside"):
        over(2, X, backward)
    with jax.named_scope("backward_edges"):
        by_sides(backward_edge, begins | ends, (backward_rows, rows_between))
    with jax.named_scope("backward_rows"):
        pl.when(jnp.logical_not(rows_between))(backward_rows)
    with jax.named_scope("finish_inside"):
        over(2, X, finish)
        finish(1, below=False)
        finish(X, above=False)
        for step in (x_state, y_state, x_middle, *y_edge, y_middle):
            step[2]()
    with jax.named_scope("finish_rows"):
        y_last[1]()
        inside_rows(finish_row)
        for edge in y_last_edge:
            edge[1]()
        edge_rows(finish_row)
    with jax.named_scope("finish_edges"):
        x_last[1]()
        for x, layer in ((0, 0), (X - 1, X + 1)):
            out_p[x] = out_p[x] + U0[layer]
            out_m[x] = out_m[x] + V0[layer]
    with jax.named_scope("wait_sends"):
        for step in (x_last, y_last, *y_last_edge):
            step[2]()


def hand_over(p_ref, m_ref, p_out, m_out, sem):
    copies = [pltpu.make_async_copy(p_ref, p_out, sem.at[0]), pltpu.make_async_copy(m_ref, m_out, sem.at[1])]
    for copy in copies:
        copy.start()
    for copy in copies:
        copy.wait()


def solution(mesh):
    nx_dev, ny_dev = mesh.shape["gx"], mesh.shape["gy"]
    split = P("gx", "gy", None)

    def on_device(*args):
        X, Y, Z = args[0].shape
        f32, i32 = jnp.float32, jnp.int32
        hbm = pl.BlockSpec(memory_space=pltpu.HBM)
        vmem = pltpu.VMEM
        copies = 4 + 2 * 9
        results = pl.pallas_call(
            functools.partial(kernel, nx_dev, ny_dev),
            out_shape=[vmem((X, Y, Z), f32)] * 2,
            in_specs=[hbm] * 9,
            out_specs=[pl.BlockSpec(memory_space=vmem)] * 2,
            scratch_shapes=(
                [vmem((X + 2, Y, Z), f32)] * 2
                + [vmem((X + 2, Y, Z), i32)] * 3
                + [vmem((X + 2, k, Y, Z), f32) for k in (2, 4, 2)]
                + [vmem((X + 2, k, 8, Z), f32) for k in (2, 4, 2)]
                + [vmem((X + 2, Y, Z), f32)] * 13
                + [pltpu.SMEM(args[7].shape, f32), pltpu.SMEM(args[8].shape, f32)]
                + [pltpu.SemaphoreType.DMA((9,))]
                + [pltpu.SemaphoreType.DMA((copies,))] * 2
                + [pltpu.SemaphoreType.REGULAR((4,))]
            ),
            compiler_params=pltpu.CompilerParams(
                collective_id=0, has_side_effects=True, vmem_limit_bytes=32 * 1024 * 1024
            ),
            name="reverse",
        )(*[pltpu.with_memory_space_constraint(arg, pltpu.HBM) for arg in args])
        results = [pltpu.with_memory_space_constraint(r, vmem) for r in results]
        return pl.pallas_call(
            hand_over,
            out_shape=[jax.ShapeDtypeStruct((X, Y, Z), f32)] * 2,
            in_specs=[pl.BlockSpec(memory_space=vmem)] * 2,
            out_specs=[hbm] * 2,
            scratch_shapes=[pltpu.SemaphoreType.DMA((2,))],
            name="hand_over",
        )(*results)

    return jax.shard_map(
        on_device, mesh=mesh, in_specs=(split,) * 7 + (P(), P()), out_specs=(split, split), check_vma=False
    )
```

```python
import functools

import jax
import jax.numpy as jnp
from jax import lax
from jax.experimental import pallas as pl
from jax.experimental.pallas import tpu as pltpu
from jax.sharding import PartitionSpec as P

mobility_step = 0.1
well_height = 1.0
coupling = 1.0
diffusion_step = 0.03

MESH = pl.DeviceIdType.MESH
RUN = 4


def pick(index, table, count):
    values = [table[k] for k in range(count)]
    bit = 1
    while len(values) > 1:
        odd = (index & bit) != 0
        values = [jnp.where(odd, values[k + 1], values[k]) for k in range(0, len(values), 2)]
        bit *= 2
    return values[0]


def local_terms(phase, jump):
    t = phase - phase * phase
    denominator = 1.0 - 2.0 * t
    rest = denominator - jump * (phase - t)
    both = 1.0 / (denominator * rest)
    inverse = rest * both
    release = denominator * (denominator * both)
    square = inverse * inverse
    slope = 2.0 * t * square
    slope_derivative = (2.0 - 4.0 * phase) * (1.0 + 2.0 * t) * (square * inverse)
    return t, slope, slope_derivative, release


def kernel(
    nx_dev, ny_dev,
    p_hbm, m_hbm, a_hbm, b_hbm, or_hbm, an_hbm, bm_hbm, st_hbm, pt_hbm,
    out_p, out_m,
    A, B, OR, AN, BM, S0, S1, S2, H0, H1, H2,
    KAP, JMP, MOV, REACH, JS0, JD0, W0, G0, K0, JS1, JD1, W1, SP1, st, pt,
    load_sem, ss, rs, ready,
):
    X, Y, Z = p_hbm.shape
    P0, M0, HP0, HM0 = S0.at[:, 0], S0.at[:, 1], H0.at[:, 0], H0.at[:, 1]
    P1, M1, U1, V1 = (S1.at[:, k] for k in range(4))
    HP1, HM1, HU1, HV1 = (H1.at[:, k] for k in range(4))
    U0, V0, HU0, HV0 = S2.at[:, 0], S2.at[:, 1], H2.at[:, 0], H2.at[:, 1]
    gx, gy = lax.axis_index("gx"), lax.axis_index("gy")
    has = {
        ("x", 0): gx > 0, ("x", 1): gx < nx_dev - 1,
        ("y", 0): gy > 0, ("y", 1): gy < ny_dev - 1,
    }
    device = {
        ("x", 0): {"gx": gx - 1}, ("x", 1): {"gx": gx + 1},
        ("y", 0): {"gy": gy - 1}, ("y", 1): {"gy": gy + 1},
    }

    at, even = lax.rem(gx, RUN), lax.rem(gy, 2) == 0
    odd, begins, ends = jnp.logical_not(even), at == 0, at == RUN - 1
    mutual = {("x", 0): has["x", 0] & begins & odd, ("x", 1): has["x", 1] & ends & odd}
    caller = begins ^ even
    calls = {
        ("x", 0): has["x", 0] & (begins | ends), ("x", 1): (has["x", 1] & (at < 2)) | mutual["x", 1],
        ("y", 0): has["y", 0] & caller, ("y", 1): has["y", 1] & caller,
    }
    called = {key: has[key] & jnp.logical_not(calls[key]) for key in has}
    asks = dict(calls)
    asks["x", 0] = calls["x", 0] & jnp.logical_not(mutual["x", 0])
    asks["x", 1] = calls["x", 1] & jnp.logical_not(mutual["x", 1])
    answer = {key: k for k, key in enumerate(has)}

    barrier = pltpu.get_barrier_semaphore()
    count = jnp.int32(0)
    for key in has:
        @pl.when(calls[key])
        def _():
            pl.semaphore_signal(barrier, inc=1, device_id=device[key], device_id_type=MESH)
        count = count + called[key].astype(jnp.int32)
    count = count + mutual["x", 1].astype(jnp.int32)

    own = pl.ds(1, X)
    loads = []
    for k, (src, dst) in enumerate((
        (p_hbm, S0.at[own, 0]), (m_hbm, S0.at[own, 1]),
        (an_hbm, AN.at[own]), (or_hbm, OR.at[own]), (bm_hbm, BM.at[own]), (st_hbm, st), (pt_hbm, pt),
        (a_hbm, A.at[own]), (b_hbm, B.at[own]),
    )):
        copy = pltpu.make_async_copy(src, dst, load_sem.at[k])
        copy.start()
        loads.append(copy)

    sems = iter(range(ss.shape[0]))

    def exchange(axis, pieces, send_if=None, arrive_if=None):
        there = {side: has[axis, side] for side in (0, 1)}
        send_if, arrive_if = send_if or there, arrive_if or there
        sends = {0: [], 1: []}
        arrivals = {0: [], 1: []}
        for down, down_to, up, up_to in pieces:
            for side, src, dst in ((0, down, down_to), (1, up, up_to)):
                if src is None:
                    continue
                k = next(sems)
                copy = pltpu.make_async_remote_copy(
                    src_ref=src, dst_ref=dst, send_sem=ss.at[k], recv_sem=rs.at[k],
                    device_id=device[axis, side], device_id_type=MESH,
                )
                sends[side].append(copy)
                arrivals[1 - side].append(copy)

        def each(groups, conditions, act):
            def run(sides=(0, 1)):
                for side in sides:
                    @pl.when(conditions[side])
                    def _():
                        for copy in groups[side]:
                            act(copy)
            return run

        return (
            each(sends, send_if, lambda copy: copy.start()),
            each(arrivals, arrive_if, lambda copy: copy.wait_recv()),
            each(sends, send_if, lambda copy: copy.wait_send()),
        )

    def x_faces(ref):
        return ref.at[1], ref.at[X + 1], ref.at[X], ref.at[0]

    inside = pl.ds(2, X - 2)

    def y_faces(ref, aside, layers=own):
        return ref.at[layers, :, 0], aside.at[layers, :, 7], ref.at[layers, :, Y - 1], aside.at[layers, :, 0]

    x_state = exchange("x", [
        (S0.at[1], S0.at[X + 1], None, None),
        (None, None, p_hbm.at[X - 1], S0.at[0, 0]),
        (None, None, m_hbm.at[X - 1], S0.at[0, 1]),
    ])
    y_state = exchange("y", [y_faces(S0, H0)])
    x_middle = exchange("x", [x_faces(S1)])
    y_edge = [exchange("y", [y_faces(S1, H1, layer)]) for layer in (1, X)]
    y_middle = exchange("y", [y_faces(S1, H1, inside)])
    x_last = exchange("x", [x_faces(S2)])
    y_last = exchange("y", [y_faces(S2, H2, inside)])
    y_last_edge = [exchange("y", [y_faces(S2, H2, layer)]) for layer in (1, X)]

    for side, layer in enumerate((0, X + 1)):
        @pl.when(jnp.logical_not(has["x", side]))
        def _():
            for ref in (S0, S1, S2):
                ref[layer] = jnp.zeros(ref.shape[1:], ref.dtype)
    for side, row in ((0, 0), (1, 7)):
        @pl.when(jnp.logical_not(has["y", side]))
        def _():
            for ref in (H0, H1):
                for layer in (1, X):
                    ref[layer, :, row:row + 1] = jnp.zeros((ref.shape[1], 1, Z), ref.dtype)

    pl.when(count > 0)(lambda: pl.semaphore_wait(barrier, count))
    for axis, side in has:
        @pl.when(called[axis, side])
        def _():
            pl.semaphore_signal(
                ready.at[answer[axis, 1 - side]], inc=1, device_id=device[axis, side], device_id_type=MESH
            )

    def wait_answer(key):
        pl.semaphore_wait(ready.at[answer[key]], 1)

    pl.when(called["x", 1] | mutual["x", 1])(lambda: x_state[0]((1,)))
    loads[0].wait()
    loads[1].wait()
    pl.when(called["x", 0])(lambda: x_state[0]((0,)))
    for side in (0, 1):
        pl.when(asks["y", side])(lambda: wait_answer(("y", side)))
        y_state[0]((side,))

    @pl.when(asks["x", 0] & ends)
    def _():
        wait_answer(("x", 0))
        x_state[0]((0,))

    for copy in loads[2:]:
        copy.wait()

    lane = lax.broadcasted_iota(jnp.int32, (8, 128), 1)
    line = lax.broadcasted_iota(jnp.int32, (8, 128), 0)
    first_lane, last_lane, first_line, last_line = lane == 0, lane == 127, line == 0, line == 7

    def shifted(parts, by, size, axis, edge):
        turned = [pltpu.roll(part, by % size, axis) for part in parts]
        return [jnp.where(edge, before, here) for before, here in zip([0.0] + turned, turned)]

    def lap(ref, i, below=True, above=True, aside=None):
        tiles = [[ref[i, a:a + 8, b:b + 128] for b in range(0, Z, 128)] for a in range(0, Y, 8)]
        result = []
        along_y = []
        for column in zip(*tiles):
            down = shifted(column, 1, 8, 0, first_line)
            up = shifted(column[::-1], -1, 8, 0, last_line)[::-1]
            along_y.append([d + u for d, u in zip(down, up)])
        if aside is not None:
            for b, column in enumerate(along_y):
                beyond = aside[i, :, 128 * b:128 * (b + 1)]
                column[0] = column[0] + jnp.where(first_line, beyond, 0.0)
                column[-1] = column[-1] + jnp.where(last_line, beyond, 0.0)
        for a, row in enumerate(tiles):
            left = shifted(row, 1, 128, 1, first_lane)
            right = shifted(row[::-1], -1, 128, 1, last_lane)[::-1]
            result.append(jnp.concatenate(
                [l + r + along_y[b][a] - 6.0 * c for b, (l, r, c) in enumerate(zip(left, right, row))], axis=1
            ))
        beside = jnp.concatenate(result, axis=0)
        if below:
            beside = beside + ref[i - 1]
        if above:
            beside = beside + ref[i + 1]
        return beside

    def tables(i):
        KAP[i] = pick(AN[i], st, st.shape[0])
        JMP[i] = 1.0 - pick(OR[i], pt, pt.shape[0])
        movable = 1.0 - BM[i].astype(jnp.float32)
        MOV[i] = movable
        REACH[i] = mobility_step * movable

    def sensitivities(at, phase):
        jump = JMP[at]
        _, slope, _, release = local_terms(phase, jump)
        spread = B[at] * (MOV[at] * release)
        U1[at] = KAP[at] * (REACH[at] * (A[at] - spread * (jump * slope)))
        V1[at] = diffusion_step * spread

    def forward(i, aside=(None, None)):
        phase, potential = P0[i], M0[i]
        jump = JMP[i]
        t, slope, slope_derivative, release = local_terms(phase, jump)
        held_slope, held_derivative = jump * slope, jump * slope_derivative
        drive = (
            KAP[i] * lap(P0, i, aside=aside[0])
            - 2.0 * well_height * t * (1.0 - 2.0 * phase)
            + coupling * held_slope * potential
        )
        step = REACH[i] * drive
        yielding = MOV[i] * release
        flux = yielding * (diffusion_step * lap(M0, i, aside=aside[1]) - held_slope * step)
        P1[i] = phase + step
        M1[i] = potential + flux
        JS0[i] = held_slope
        JD0[i] = held_derivative
        W0[i] = yielding
        G0[i] = well_height * (12.0 * t - 2.0) + coupling * held_derivative * potential
        K0[i] = held_slope * flux - held_derivative * step
        sensitivities(i, phase + step)

    def forward_row(i, row, aside):
        here, away = (i, slice(row, row + 1)), (i, slice(aside, aside + 1))
        step = REACH[here] * KAP[here] * HP0[away]
        flux = W0[here] * (diffusion_step * HM0[away] - JS0[here] * step)
        phase = P1[here] + step
        P1[here] = phase
        M1[here] = M1[here] + flux
        K0[here] = K0[here] + JS0[here] * flux - JD0[here] * step
        sensitivities(here, phase)

    def backward(i, aside=(None, None, None, None)):
        x = i - 1
        phase, potential = P1[i], M1[i]
        jump, reach = JMP[i], REACH[i]
        t, slope, slope_derivative, release = local_terms(phase, jump)
        held_slope, held_derivative = jump * slope, jump * slope_derivative
        drive = (
            KAP[i] * lap(P1, i, aside=aside[0])
            - 2.0 * well_height * t * (1.0 - 2.0 * phase)
            + coupling * held_slope * potential
        )
        step = reach * drive
        yielding = MOV[i] * release
        flux = yielding * (diffusion_step * lap(M1, i, aside=aside[1]) - held_slope * step)
        gain = well_height * (12.0 * t - 2.0) + coupling * held_derivative * potential
        keep = held_slope * flux - held_derivative * step
        spread = B[i] * yielding
        pull = reach * (A[i] - spread * held_slope)
        JS1[i] = held_slope
        JD1[i] = held_derivative
        W1[i] = yielding
        SP1[i] = spread
        bar_p = A[i] + pull * gain + spread * keep + lap(U1, i, aside=aside[2])
        bar_m = B[i] + coupling * held_slope * pull + lap(V1, i, aside=aside[3])
        spread = bar_m * W0[i]
        pull = reach * (bar_p - spread * JS0[i])
        U0[i] = KAP[i] * pull
        V0[i] = diffusion_step * spread
        out_p[x] = bar_p + pull * G0[i] + spread * K0[i]
        out_m[x] = bar_m + coupling * JS0[i] * pull

    def backward_row(i, row, aside):
        at, here, away = (i - 1, slice(row, row + 1)), (i, slice(row, row + 1)), (i, slice(aside, aside + 1))
        step = REACH[here] * KAP[here] * HP1[away]
        flux = W1[here] * (diffusion_step * HM1[away] - JS1[here] * step)
        bar_p = SP1[here] * (JS1[here] * flux - JD1[here] * step) + HU1[away]
        bar_m = HV1[away]
        spread = bar_m * W0[here]
        pull = REACH[here] * (bar_p - spread * JS0[here])
        U0[here] = U0[here] + KAP[here] * pull
        V0[here] = V0[here] + diffusion_step * spread
        out_p[at] = out_p[at] + (bar_p + pull * G0[here] + spread * K0[here])
        out_m[at] = out_m[at] + (bar_m + coupling * JS0[here] * pull)

    def finish(i, **sides):
        out_p[i - 1] = out_p[i - 1] + lap(U0, i, **sides)
        out_m[i - 1] = out_m[i - 1] + lap(V0, i, **sides)

    def finish_row(i, row, aside):
        at, away = (i - 1, slice(row, row + 1)), (i, slice(aside, aside + 1))
        out_p[at] = out_p[at] + HU0[away]
        out_m[at] = out_m[at] + HV0[away]

    def over(low, high, body, unroll=2):
        def step(x, carry):
            body(x)
            return carry
        lax.fori_loop(low, high, step, 0, unroll=unroll)

    def edges(body):
        over(0, 2, lambda k: body(1 + k * (X - 1)))

    def by_rows(run, body):
        for side, row, aside in ((0, 0, 0), (1, Y - 1, 7)):
            @pl.when(has["y", side])
            def _():
                run(lambda x: body(x, row, aside))

    def inside_rows(body):
        by_rows(lambda act: over(2, X, act, 2), body)

    def edge_rows(body):
        by_rows(edges, body)

    with jax.named_scope("tables"):
        over(1, X + 1, tables)
    with jax.named_scope("forward_inside"):
        over(2, X, forward)
        @pl.when(asks["x", 1])
        def _():
            wait_answer(("x", 1))
            x_state[0]((1,))

        @pl.when(asks["x", 0] & begins)
        def _():
            wait_answer(("x", 0))
            x_state[0]((0,))

        @pl.when(mutual["x", 0])
        def _():
            pl.semaphore_wait(barrier, 1)
            x_state[0]((0,))

    def by_sides(body, upper_first, between=None):
        def do_between(order):
            if between is not None:
                pl.when(order & between[1])(between[0])

        lower_first = jnp.logical_not(upper_first)
        pl.when(upper_first)(lambda: body(1, X))
        do_between(upper_first)
        body(0, 1)
        do_between(lower_first)
        pl.when(lower_first)(lambda: body(1, X))

    after = (gy >= ny_dev // 2) | odd
    let_go = {0: begins & after, 1: ends & after}

    def forward_edge(side, layer):
        x_state[1]((side,))
        forward(layer, (HP0, HM0))
        pl.when(jnp.logical_not(let_go[side]))(lambda: x_middle[0]((side,)))
        y_edge[side][0]()

    def backward_edge(side, layer):
        y_edge[side][1]()
        x_middle[1]((side,))
        backward(layer, (HP1, HM1, HU1, HV1))
        x_last[0]((side,))
        y_last_edge[side][0]()

    def backward_rows():
        y_middle[1]()
        inside_rows(backward_row)
        y_last[0]()

    rows_between = at < 2

    with jax.named_scope("forward_edges"):
        y_state[1]()
        by_sides(forward_edge, begins)
    with jax.named_scope("forward_rows"):
        inside_rows(forward_row)
        for side in (0, 1):
            pl.when(let_go[side])(lambda: x_middle[0]((side,)))
        rows_later = ends & ((gy == ny_dev // 2 - 1) | (gy == ny_dev // 2))
        pl.when(jnp.logical_not(rows_later))(lambda: y_middle[0]())
    with jax.named_scope("backward_inside"):
        over(2, X, backward)
        pl.when(rows_later)(lambda: y_middle[0]())
    with jax.named_scope("backward_edges"):
        by_sides(backward_edge, begins | ends, (backward_rows, rows_between))
    with jax.named_scope("backward_rows"):
        pl.when(jnp.logical_not(rows_between))(backward_rows)
    with jax.named_scope("finish_inside"):
        over(2, X, finish)
        finish(1, below=False)
        finish(X, above=False)
        for step in (x_state, y_state, x_middle, *y_edge, y_middle):
            step[2]()
    with jax.named_scope("finish_rows"):
        y_last[1]()
        inside_rows(finish_row)
        for edge in y_last_edge:
            edge[1]()
        edge_rows(finish_row)
    with jax.named_scope("finish_edges"):
        x_last[1]()
        for x, layer in ((0, 0), (X - 1, X + 1)):
            out_p[x] = out_p[x] + U0[layer]
            out_m[x] = out_m[x] + V0[layer]
    with jax.named_scope("wait_sends"):
        for step in (x_last, y_last, *y_last_edge):
            step[2]()


def hand_over(p_ref, m_ref, p_out, m_out, sem):
    copies = [pltpu.make_async_copy(p_ref, p_out, sem.at[0]), pltpu.make_async_copy(m_ref, m_out, sem.at[1])]
    for copy in copies:
        copy.start()
    for copy in copies:
        copy.wait()


def solution(mesh):
    nx_dev, ny_dev = mesh.shape["gx"], mesh.shape["gy"]
    split = P("gx", "gy", None)

    def on_device(*args):
        X, Y, Z = args[0].shape
        f32, i32 = jnp.float32, jnp.int32
        hbm = pl.BlockSpec(memory_space=pltpu.HBM)
        vmem = pltpu.VMEM
        copies = 4 + 2 * 9
        results = pl.pallas_call(
            functools.partial(kernel, nx_dev, ny_dev),
            out_shape=[vmem((X, Y, Z), f32)] * 2,
            in_specs=[hbm] * 9,
            out_specs=[pl.BlockSpec(memory_space=vmem)] * 2,
            scratch_shapes=(
                [vmem((X + 2, Y, Z), f32)] * 2
                + [vmem((X + 2, Y, Z), i32)] * 3
                + [vmem((X + 2, k, Y, Z), f32) for k in (2, 4, 2)]
                + [vmem((X + 2, k, 8, Z), f32) for k in (2, 4, 2)]
                + [vmem((X + 2, Y, Z), f32)] * 13
                + [pltpu.SMEM(args[7].shape, f32), pltpu.SMEM(args[8].shape, f32)]
                + [pltpu.SemaphoreType.DMA((9,))]
                + [pltpu.SemaphoreType.DMA((copies,))] * 2
                + [pltpu.SemaphoreType.REGULAR((4,))]
            ),
            compiler_params=pltpu.CompilerParams(
                collective_id=0, has_side_effects=True, vmem_limit_bytes=32 * 1024 * 1024
            ),
            name="reverse",
        )(*[pltpu.with_memory_space_constraint(arg, pltpu.HBM) for arg in args])
        results = [pltpu.with_memory_space_constraint(r, vmem) for r in results]
        return pl.pallas_call(
            hand_over,
            out_shape=[jax.ShapeDtypeStruct((X, Y, Z), f32)] * 2,
            in_specs=[pl.BlockSpec(memory_space=vmem)] * 2,
            out_specs=[hbm] * 2,
            scratch_shapes=[pltpu.SemaphoreType.DMA((2,))],
            name="hand_over",
        )(*results)

    return jax.shard_map(
        on_device, mesh=mesh, in_specs=(split,) * 7 + (P(), P()), out_specs=(split, split), check_vma=False
    )
```

```python
import functools

import jax
import jax.numpy as jnp
from jax import lax
from jax.experimental import pallas as pl
from jax.experimental.pallas import tpu as pltpu
from jax.sharding import PartitionSpec as P

mobility_step = 0.1
well_height = 1.0
coupling = 1.0
diffusion_step = 0.03

MESH = pl.DeviceIdType.MESH
RUN = 4


def pick(index, table, count):
    values = [table[k] for k in range(count)]
    bit = 1
    while len(values) > 1:
        odd = (index & bit) != 0
        values = [jnp.where(odd, values[k + 1], values[k]) for k in range(0, len(values), 2)]
        bit *= 2
    return values[0]


def local_terms(phase, jump):
    t = phase - phase * phase
    denominator = 1.0 - 2.0 * t
    rest = denominator - jump * (phase - t)
    both = 1.0 / (denominator * rest)
    inverse = rest * both
    release = denominator * (denominator * both)
    square = inverse * inverse
    slope = 2.0 * t * square
    slope_derivative = (2.0 - 4.0 * phase) * (1.0 + 2.0 * t) * (square * inverse)
    return t, slope, slope_derivative, release


def kernel(
    nx_dev, ny_dev,
    p_hbm, m_hbm, a_hbm, b_hbm, or_hbm, an_hbm, bm_hbm, st_hbm, pt_hbm,
    out_p, out_m,
    A, B, OR, AN, BM, S0, S1, S2, H0, H1, H2,
    KAP, JMP, MOV, REACH, JS0, JD0, W0, G0, K0, JS1, JD1, W1, SP1, st, pt,
    load_sem, ss, rs, ready,
):
    X, Y, Z = p_hbm.shape
    P0, M0, HP0, HM0 = S0.at[:, 0], S0.at[:, 1], H0.at[:, 0], H0.at[:, 1]
    P1, M1, U1, V1 = (S1.at[:, k] for k in range(4))
    HP1, HM1, HU1, HV1 = (H1.at[:, k] for k in range(4))
    U0, V0, HU0, HV0 = S2.at[:, 0], S2.at[:, 1], H2.at[:, 0], H2.at[:, 1]
    gx, gy = lax.axis_index("gx"), lax.axis_index("gy")
    has = {
        ("x", 0): gx > 0, ("x", 1): gx < nx_dev - 1,
        ("y", 0): gy > 0, ("y", 1): gy < ny_dev - 1,
    }
    device = {
        ("x", 0): {"gx": gx - 1}, ("x", 1): {"gx": gx + 1},
        ("y", 0): {"gy": gy - 1}, ("y", 1): {"gy": gy + 1},
    }

    at, even = lax.rem(gx, RUN), lax.rem(gy, 2) == 0
    odd, begins, ends = jnp.logical_not(even), at == 0, at == RUN - 1
    mutual = {("x", 0): has["x", 0] & begins & odd, ("x", 1): has["x", 1] & ends & odd}
    half = ny_dev // 2
    calls_down = (begins & odd) | (jnp.logical_not(begins) & (gy == half))
    calls_up = (begins & odd) | (jnp.logical_not(begins) & (gy != half - 1))
    calls = {
        ("x", 0): has["x", 0] & (begins | ends), ("x", 1): (has["x", 1] & (at < 2)) | mutual["x", 1],
        ("y", 0): has["y", 0] & calls_down, ("y", 1): has["y", 1] & calls_up,
    }
    called = {key: has[key] & jnp.logical_not(calls[key]) for key in has}
    asks = dict(calls)
    asks["x", 0] = calls["x", 0] & jnp.logical_not(mutual["x", 0])
    asks["x", 1] = calls["x", 1] & jnp.logical_not(mutual["x", 1])
    answer = {key: k for k, key in enumerate(has)}

    barrier = pltpu.get_barrier_semaphore()
    count = jnp.int32(0)
    for key in has:
        @pl.when(calls[key])
        def _():
            pl.semaphore_signal(barrier, inc=1, device_id=device[key], device_id_type=MESH)
        count = count + called[key].astype(jnp.int32)
    count = count + mutual["x", 1].astype(jnp.int32)

    own = pl.ds(1, X)
    loads = []
    for k, (src, dst) in enumerate((
        (p_hbm, S0.at[own, 0]), (m_hbm, S0.at[own, 1]),
        (an_hbm, AN.at[own]), (or_hbm, OR.at[own]), (bm_hbm, BM.at[own]), (st_hbm, st), (pt_hbm, pt),
        (a_hbm, A.at[own]), (b_hbm, B.at[own]),
    )):
        copy = pltpu.make_async_copy(src, dst, load_sem.at[k])
        copy.start()
        loads.append(copy)

    sems = iter(range(ss.shape[0]))

    def exchange(axis, pieces, send_if=None, arrive_if=None):
        there = {side: has[axis, side] for side in (0, 1)}
        send_if, arrive_if = send_if or there, arrive_if or there
        sends = {0: [], 1: []}
        arrivals = {0: [], 1: []}
        for down, down_to, up, up_to in pieces:
            for side, src, dst in ((0, down, down_to), (1, up, up_to)):
                if src is None:
                    continue
                k = next(sems)
                copy = pltpu.make_async_remote_copy(
                    src_ref=src, dst_ref=dst, send_sem=ss.at[k], recv_sem=rs.at[k],
                    device_id=device[axis, side], device_id_type=MESH,
                )
                sends[side].append(copy)
                arrivals[1 - side].append(copy)

        def each(groups, conditions, act):
            def run(sides=(0, 1)):
                for side in sides:
                    @pl.when(conditions[side])
                    def _():
                        for copy in groups[side]:
                            act(copy)
            return run

        return (
            each(sends, send_if, lambda copy: copy.start()),
            each(arrivals, arrive_if, lambda copy: copy.wait_recv()),
            each(sends, send_if, lambda copy: copy.wait_send()),
        )

    def x_faces(ref):
        return ref.at[1], ref.at[X + 1], ref.at[X], ref.at[0]

    inside = pl.ds(2, X - 2)

    def y_faces(ref, aside, layers=own):
        return ref.at[layers, :, 0], aside.at[layers, :, 7], ref.at[layers, :, Y - 1], aside.at[layers, :, 0]

    x_state = exchange("x", [
        (S0.at[1], S0.at[X + 1], None, None),
        (None, None, p_hbm.at[X - 1], S0.at[0, 0]),
        (None, None, m_hbm.at[X - 1], S0.at[0, 1]),
    ])
    y_state = exchange("y", [y_faces(S0, H0)])
    x_middle = exchange("x", [x_faces(S1)])
    y_edge = [exchange("y", [y_faces(S1, H1, layer)]) for layer in (1, X)]
    y_middle = exchange("y", [y_faces(S1, H1, inside)])
    x_last = exchange("x", [x_faces(S2)])
    y_last = exchange("y", [y_faces(S2, H2, inside)])
    y_last_edge = [exchange("y", [y_faces(S2, H2, layer)]) for layer in (1, X)]

    for side, layer in enumerate((0, X + 1)):
        @pl.when(jnp.logical_not(has["x", side]))
        def _():
            for ref in (S0, S1, S2):
                ref[layer] = jnp.zeros(ref.shape[1:], ref.dtype)
    for side, row in ((0, 0), (1, 7)):
        @pl.when(jnp.logical_not(has["y", side]))
        def _():
            for ref in (H0, H1):
                for layer in (1, X):
                    ref[layer, :, row:row + 1] = jnp.zeros((ref.shape[1], 1, Z), ref.dtype)

    pl.when(count > 0)(lambda: pl.semaphore_wait(barrier, count))
    for axis, side in has:
        @pl.when(called[axis, side])
        def _():
            pl.semaphore_signal(
                ready.at[answer[axis, 1 - side]], inc=1, device_id=device[axis, side], device_id_type=MESH
            )

    def wait_answer(key):
        pl.semaphore_wait(ready.at[answer[key]], 1)

    pl.when(called["x", 1] | mutual["x", 1])(lambda: x_state[0]((1,)))
    loads[0].wait()
    loads[1].wait()
    pl.when(called["x", 0])(lambda: x_state[0]((0,)))
    for side in (0, 1):
        pl.when(asks["y", side])(lambda: wait_answer(("y", side)))
        y_state[0]((side,))

    @pl.when(asks["x", 0] & ends)
    def _():
        wait_answer(("x", 0))
        x_state[0]((0,))

    for copy in loads[2:]:
        copy.wait()

    lane = lax.broadcasted_iota(jnp.int32, (8, 128), 1)
    line = lax.broadcasted_iota(jnp.int32, (8, 128), 0)
    first_lane, last_lane, first_line, last_line = lane == 0, lane == 127, line == 0, line == 7

    def shifted(parts, by, size, axis, edge):
        turned = [pltpu.roll(part, by % size, axis) for part in parts]
        return [jnp.where(edge, before, here) for before, here in zip([0.0] + turned, turned)]

    def lap(ref, i, below=True, above=True, aside=None):
        tiles = [[ref[i, a:a + 8, b:b + 128] for b in range(0, Z, 128)] for a in range(0, Y, 8)]
        result = []
        along_y = []
        for column in zip(*tiles):
            down = shifted(column, 1, 8, 0, first_line)
            up = shifted(column[::-1], -1, 8, 0, last_line)[::-1]
            along_y.append([d + u for d, u in zip(down, up)])
        if aside is not None:
            for b, column in enumerate(along_y):
                beyond = aside[i, :, 128 * b:128 * (b + 1)]
                column[0] = column[0] + jnp.where(first_line, beyond, 0.0)
                column[-1] = column[-1] + jnp.where(last_line, beyond, 0.0)
        for a, row in enumerate(tiles):
            left = shifted(row, 1, 128, 1, first_lane)
            right = shifted(row[::-1], -1, 128, 1, last_lane)[::-1]
            result.append(jnp.concatenate(
                [l + r + along_y[b][a] - 6.0 * c for b, (l, r, c) in enumerate(zip(left, right, row))], axis=1
            ))
        beside = jnp.concatenate(result, axis=0)
        if below:
            beside = beside + ref[i - 1]
        if above:
            beside = beside + ref[i + 1]
        return beside

    def tables(i):
        KAP[i] = pick(AN[i], st, st.shape[0])
        JMP[i] = 1.0 - pick(OR[i], pt, pt.shape[0])
        movable = 1.0 - BM[i].astype(jnp.float32)
        MOV[i] = movable
        REACH[i] = mobility_step * movable

    def sensitivities(at, phase):
        jump = JMP[at]
        _, slope, _, release = local_terms(phase, jump)
        spread = B[at] * (MOV[at] * release)
        U1[at] = KAP[at] * (REACH[at] * (A[at] - spread * (jump * slope)))
        V1[at] = diffusion_step * spread

    def forward(i, aside=(None, None)):
        phase, potential = P0[i], M0[i]
        jump = JMP[i]
        t, slope, slope_derivative, release = local_terms(phase, jump)
        held_slope, held_derivative = jump * slope, jump * slope_derivative
        drive = (
            KAP[i] * lap(P0, i, aside=aside[0])
            - 2.0 * well_height * t * (1.0 - 2.0 * phase)
            + coupling * held_slope * potential
        )
        step = REACH[i] * drive
        yielding = MOV[i] * release
        flux = yielding * (diffusion_step * lap(M0, i, aside=aside[1]) - held_slope * step)
        P1[i] = phase + step
        M1[i] = potential + flux
        JS0[i] = held_slope
        JD0[i] = held_derivative
        W0[i] = yielding
        G0[i] = well_height * (12.0 * t - 2.0) + coupling * held_derivative * potential
        K0[i] = held_slope * flux - held_derivative * step
        sensitivities(i, phase + step)

    def forward_row(i, row, aside):
        here, away = (i, slice(row, row + 1)), (i, slice(aside, aside + 1))
        step = REACH[here] * KAP[here] * HP0[away]
        flux = W0[here] * (diffusion_step * HM0[away] - JS0[here] * step)
        phase = P1[here] + step
        P1[here] = phase
        M1[here] = M1[here] + flux
        K0[here] = K0[here] + JS0[here] * flux - JD0[here] * step
        sensitivities(here, phase)

    def backward(i, aside=(None, None, None, None)):
        x = i - 1
        phase, potential = P1[i], M1[i]
        jump, reach = JMP[i], REACH[i]
        t, slope, slope_derivative, release = local_terms(phase, jump)
        held_slope, held_derivative = jump * slope, jump * slope_derivative
        drive = (
            KAP[i] * lap(P1, i, aside=aside[0])
            - 2.0 * well_height * t * (1.0 - 2.0 * phase)
            + coupling * held_slope * potential
        )
        step = reach * drive
        yielding = MOV[i] * release
        flux = yielding * (diffusion_step * lap(M1, i, aside=aside[1]) - held_slope * step)
        gain = well_height * (12.0 * t - 2.0) + coupling * held_derivative * potential
        keep = held_slope * flux - held_derivative * step
        spread = B[i] * yielding
        pull = reach * (A[i] - spread * held_slope)
        JS1[i] = held_slope
        JD1[i] = held_derivative
        W1[i] = yielding
        SP1[i] = spread
        bar_p = A[i] + pull * gain + spread * keep + lap(U1, i, aside=aside[2])
        bar_m = B[i] + coupling * held_slope * pull + lap(V1, i, aside=aside[3])
        spread = bar_m * W0[i]
        pull = reach * (bar_p - spread * JS0[i])
        U0[i] = KAP[i] * pull
        V0[i] = diffusion_step * spread
        out_p[x] = bar_p + pull * G0[i] + spread * K0[i]
        out_m[x] = bar_m + coupling * JS0[i] * pull

    def backward_row(i, row, aside):
        at, here, away = (i - 1, slice(row, row + 1)), (i, slice(row, row + 1)), (i, slice(aside, aside + 1))
        step = REACH[here] * KAP[here] * HP1[away]
        flux = W1[here] * (diffusion_step * HM1[away] - JS1[here] * step)
        bar_p = SP1[here] * (JS1[here] * flux - JD1[here] * step) + HU1[away]
        bar_m = HV1[away]
        spread = bar_m * W0[here]
        pull = REACH[here] * (bar_p - spread * JS0[here])
        U0[here] = U0[here] + KAP[here] * pull
        V0[here] = V0[here] + diffusion_step * spread
        out_p[at] = out_p[at] + (bar_p + pull * G0[here] + spread * K0[here])
        out_m[at] = out_m[at] + (bar_m + coupling * JS0[here] * pull)

    def finish(i, **sides):
        out_p[i - 1] = out_p[i - 1] + lap(U0, i, **sides)
        out_m[i - 1] = out_m[i - 1] + lap(V0, i, **sides)

    def finish_row(i, row, aside):
        at, away = (i - 1, slice(row, row + 1)), (i, slice(aside, aside + 1))
        out_p[at] = out_p[at] + HU0[away]
        out_m[at] = out_m[at] + HV0[away]

    def over(low, high, body, unroll=2):
        def step(x, carry):
            body(x)
            return carry
        lax.fori_loop(low, high, step, 0, unroll=unroll)

    def edges(body):
        over(0, 2, lambda k: body(1 + k * (X - 1)))

    def by_rows(run, body):
        for side, row, aside in ((0, 0, 0), (1, Y - 1, 7)):
            @pl.when(has["y", side])
            def _():
                run(lambda x: body(x, row, aside))

    def inside_rows(body):
        by_rows(lambda act: over(2, X, act, 2), body)

    def edge_rows(body):
        by_rows(edges, body)

    with jax.named_scope("tables"):
        over(1, X + 1, tables)
    with jax.named_scope("forward_inside"):
        over(2, X, forward)
        @pl.when(asks["x", 1])
        def _():
            wait_answer(("x", 1))
            x_state[0]((1,))

        @pl.when(asks["x", 0] & begins)
        def _():
            wait_answer(("x", 0))
            x_state[0]((0,))

        @pl.when(mutual["x", 0])
        def _():
            pl.semaphore_wait(barrier, 1)
            x_state[0]((0,))

    def by_sides(body, upper_first, between=None):
        def do_between(order):
            if between is not None:
                pl.when(order & between[1])(between[0])

        lower_first = jnp.logical_not(upper_first)
        pl.when(upper_first)(lambda: body(1, X))
        do_between(upper_first)
        body(0, 1)
        do_between(lower_first)
        pl.when(lower_first)(lambda: body(1, X))

    after = (gy >= half) | odd
    let_go = {0: begins & (gy >= half), 1: ends & after}

    def forward_edge(side, layer):
        x_state[1]((side,))
        forward(layer, (HP0, HM0))
        pl.when(jnp.logical_not(let_go[side]))(lambda: x_middle[0]((side,)))
        y_edge[side][0]()

    def backward_edge(side, layer):
        y_edge[side][1]()
        x_middle[1]((side,))
        backward(layer, (HP1, HM1, HU1, HV1))
        x_last[0]((side,))
        y_last_edge[side][0]()

    def backward_rows():
        y_middle[1]()
        inside_rows(backward_row)
        y_last[0]()

    rows_between = at < 2

    middle = (gy == half - 1) | (gy == half)
    rows_later = ends & middle
    rows_early = begins & (jnp.logical_not(after) | middle)

    def forward_rows():
        inside_rows(forward_row)
        pl.when(jnp.logical_not(rows_later))(lambda: y_middle[0]())

    with jax.named_scope("forward_edges"):
        y_state[1]()
        by_sides(forward_edge, begins, (forward_rows, rows_early))
    with jax.named_scope("forward_rows"):
        pl.when(jnp.logical_not(rows_early))(forward_rows)
        for side in (0, 1):
            pl.when(let_go[side])(lambda: x_middle[0]((side,)))
    with jax.named_scope("backward_inside"):
        over(2, X, backward)
        pl.when(rows_later)(lambda: y_middle[0]())
    with jax.named_scope("backward_edges"):
        by_sides(backward_edge, begins | ends, (backward_rows, rows_between))
    with jax.named_scope("backward_rows"):
        pl.when(jnp.logical_not(rows_between))(backward_rows)
    with jax.named_scope("finish_inside"):
        over(2, X, finish)
        finish(1, below=False)
        finish(X, above=False)
        for step in (x_state, y_state, x_middle, *y_edge, y_middle):
            step[2]()
    with jax.named_scope("finish_rows"):
        y_last[1]()
        inside_rows(finish_row)
        for edge in y_last_edge:
            edge[1]()
        edge_rows(finish_row)
    with jax.named_scope("finish_edges"):
        x_last[1]()
        for x, layer in ((0, 0), (X - 1, X + 1)):
            out_p[x] = out_p[x] + U0[layer]
            out_m[x] = out_m[x] + V0[layer]
    with jax.named_scope("wait_sends"):
        for step in (x_last, y_last, *y_last_edge):
            step[2]()


def hand_over(p_ref, m_ref, p_out, m_out, sem):
    copies = [pltpu.make_async_copy(p_ref, p_out, sem.at[0]), pltpu.make_async_copy(m_ref, m_out, sem.at[1])]
    for copy in copies:
        copy.start()
    for copy in copies:
        copy.wait()


def solution(mesh):
    nx_dev, ny_dev = mesh.shape["gx"], mesh.shape["gy"]
    split = P("gx", "gy", None)

    def on_device(*args):
        X, Y, Z = args[0].shape
        f32, i32 = jnp.float32, jnp.int32
        hbm = pl.BlockSpec(memory_space=pltpu.HBM)
        vmem = pltpu.VMEM
        copies = 4 + 2 * 9
        results = pl.pallas_call(
            functools.partial(kernel, nx_dev, ny_dev),
            out_shape=[vmem((X, Y, Z), f32)] * 2,
            in_specs=[hbm] * 9,
            out_specs=[pl.BlockSpec(memory_space=vmem)] * 2,
            scratch_shapes=(
                [vmem((X + 2, Y, Z), f32)] * 2
                + [vmem((X + 2, Y, Z), i32)] * 3
                + [vmem((X + 2, k, Y, Z), f32) for k in (2, 4, 2)]
                + [vmem((X + 2, k, 8, Z), f32) for k in (2, 4, 2)]
                + [vmem((X + 2, Y, Z), f32)] * 13
                + [pltpu.SMEM(args[7].shape, f32), pltpu.SMEM(args[8].shape, f32)]
                + [pltpu.SemaphoreType.DMA((9,))]
                + [pltpu.SemaphoreType.DMA((copies,))] * 2
                + [pltpu.SemaphoreType.REGULAR((4,))]
            ),
            compiler_params=pltpu.CompilerParams(
                collective_id=0, has_side_effects=True, vmem_limit_bytes=32 * 1024 * 1024
            ),
            name="reverse",
        )(*[pltpu.with_memory_space_constraint(arg, pltpu.HBM) for arg in args])
        results = [pltpu.with_memory_space_constraint(r, vmem) for r in results]
        return pl.pallas_call(
            hand_over,
            out_shape=[jax.ShapeDtypeStruct((X, Y, Z), f32)] * 2,
            in_specs=[pl.BlockSpec(memory_space=vmem)] * 2,
            out_specs=[hbm] * 2,
            scratch_shapes=[pltpu.SemaphoreType.DMA((2,))],
            name="hand_over",
        )(*results)

    return jax.shard_map(
        on_device, mesh=mesh, in_specs=(split,) * 7 + (P(), P()), out_specs=(split, split), check_vma=False
    )
```
